512 devices in a mesh: group: 8 (over x, core), dev: 64 (over z, y).
Axes of the slice: x: 4, y: 4, z: 16, core: 2. Of those that a mesh axis runs over, the one named last changes fastest.
Arguments:
- cam_jac: float32 [2, 9, 8, 262144], P(None, None, None, ('group', 'dev')), may hold values from -6 to 6
- lm_jac: float32 [2, 3, 8, 262144], P(None, None, None, ('group', 'dev')), may hold values from -6 to 6
- resid: float32 [2, 8, 262144], P(None, None, ('group', 'dev')), may hold values from -6 to 6
- cam_index: int32 [8, 262144], P(None, ('group', 'dev')), may hold values from 0 to 8191
Outputs:
- camera_step: float32 [9, 8192], P(None, 'dev')
- camera_residual: float32 [9, 8192], P(None, 'dev')
- landmark_step: float32 [3, 262144], P(None, ('group', 'dev'))
The draws below stay inside these ranges and needn't reach their ends.
Inputs may be any that keep to these rules, and one draw needn't show every extreme that they name: `cam_index`: every observation names one of the 8192 cameras.
All inputs are finite; a program needn't handle non-finite values.
Results may differ from the reference program's by a relative error of at most 0.0003.
Values sent between devices are 32-bit elements; how exact they have to be, the bound alone decides.
A program may use at most 64 MiB of HBM per device.

```python
import math
import jax
import jax.numpy as jnp
import numpy as np

K = 8
ITERS = 2
LANDMARKS = 262144
CAMERAS = 8192


def touch_ends(result, rng, least, high):
    longest = result.shape.index(max(result.shape))
    spots = []
    for shift in (0, 1):
        where = [jax.random.randint(jax.random.fold_in(rng, axis), (), 0, length) for axis, length in enumerate(result.shape)]
        where[longest] = (where[longest] + shift) % result.shape[longest]
        spots.append(tuple(where))
    return result.at[spots[0]].set(least).at[spots[1]].set(high)


def block_levels(own_key, dims, pieces, smallest, top_value):
    level = 1.0
    for axis_at, shards_of in pieces:
        steps = jax.random.uniform(jax.random.fold_in(jax.random.fold_in(own_key, 6), axis_at), (shards_of,), jnp.float32, smallest / len(pieces), top_value / len(pieces))
        level = level * jnp.repeat(jnp.exp(steps), dims[axis_at] // shards_of).reshape((-1,) + (1,) * (len(dims) - 1 - axis_at))
    return level


def rank_bounds(count, skew):
    portions = [(1 << 20) // math.isqrt(rank ** skew) + 1 for rank in range(1, count + 1)]
    spread = 1 + sum(portions) // (1 << 30)
    return np.cumsum(np.array([max(1, weight // spread) for weight in portions]))


def ranked(key, dims, amount, lean):
    listing = rank_bounds(amount, lean)
    lot = jax.random.randint(jax.random.fold_in(key, 1), dims, 0, int(listing[amount - 1]))
    standing = jnp.searchsorted(jnp.asarray(listing, jnp.int32), lot, side="right")
    return jax.random.permutation(jax.random.fold_in(key, 2), amount)[standing].astype(jnp.int32)


def centred(stream_key, extent, scale, reach, shards=(), held_as=jnp.bfloat16):
    result = jax.random.normal(stream_key, extent, jnp.float32) * scale
    if len(shards) > 0:
        result = block_levels(stream_key, extent, shards, -0.22, 0.18) * result
    return jnp.clip(result, min=-reach, max=reach).astype(held_as)


def setup_inputs(seed: int = 0) -> dict:
    splits = jax.random.split(jax.random.key(seed), 5)
    return {
        "cam_jac": centred(splits[0], (2, 9, K, LANDMARKS), 1.0, 6.0, ((3, 512),), jnp.float32),
        "lm_jac": centred(splits[1], (2, 3, K, LANDMARKS), 1.0, 6.0, ((3, 512),), jnp.float32),
        "resid": centred(splits[2], (2, K, LANDMARKS), 1.0, 6.0, ((2, 512),), jnp.float32),
        "cam_index": touch_ends(ranked(splits[3], (K, LANDMARKS), CAMERAS, 2), jax.random.fold_in(splits[3], 3), 0, CAMERAS - 1).astype(jnp.int32),
    }


DAMPING = 1.0


def landmark_inverse(lm_jac):
    def entry(first, second):
        return jnp.sum(lm_jac[:, first] * lm_jac[:, second], axis=(0, 1))
    w_00 = entry(0, 0) + DAMPING
    w_11 = entry(1, 1) + DAMPING
    w_22 = entry(2, 2) + DAMPING
    w_01 = entry(0, 1)
    w_02 = entry(0, 2)
    w_12 = entry(1, 2)
    cof_00 = w_11 * w_22 - w_12 * w_12
    cof_01 = w_02 * w_12 - w_01 * w_22
    cof_02 = w_01 * w_12 - w_02 * w_11
    cof_11 = w_00 * w_22 - w_02 * w_02
    cof_12 = w_01 * w_02 - w_00 * w_12
    cof_22 = w_00 * w_11 - w_01 * w_01
    determinant = w_00 * cof_00 + w_01 * cof_01 + w_02 * cof_02
    rows = [jnp.stack([cof_00, cof_01, cof_02]), jnp.stack([cof_01, cof_11, cof_12]), jnp.stack([cof_02, cof_12, cof_22])]
    return jnp.stack(rows) / determinant[None, None]


def apply_inverse(inverse, vector):
    return jnp.sum(inverse * vector[None], axis=1)


def landmark_side(lm_jac, values):
    return jnp.sum(lm_jac * values[:, None], axis=(0, 2))


def back_project(lm_jac, landmark):
    return jnp.sum(lm_jac * landmark[None, :, None, :], axis=1)


def camera_apply(cam_jac, cam_values):
    return jnp.sum(cam_jac * cam_values[None], axis=1)


def camera_transpose(cam_jac, errors):
    return jnp.sum(cam_jac * errors[:, None], axis=0)


def to_cameras(values, cam_index, total_cams):
    flat_index = cam_index.reshape(-1)

    def one_row(column):
        return jax.ops.segment_sum(column, flat_index, num_segments=total_cams)

    return jax.vmap(one_row)(values.reshape(9, -1))


def schur_obs(cam_jac, lm_jac, inverse, cam_values):
    applied = camera_apply(cam_jac, cam_values)
    landmark = apply_inverse(inverse, landmark_side(lm_jac, applied))
    return camera_transpose(cam_jac, applied - back_project(lm_jac, landmark))


def reference(cam_jac, lm_jac, resid, cam_index):
    inverse = landmark_inverse(lm_jac)
    land_rhs = apply_inverse(inverse, landmark_side(lm_jac, resid))
    errors = resid - back_project(lm_jac, land_rhs)
    gradient = to_cameras(camera_transpose(cam_jac, errors), cam_index, CAMERAS)
    diagonal = to_cameras(jnp.sum(cam_jac * cam_jac, axis=0), cam_index, CAMERAS) + DAMPING

    def product(direction):
        cam_values = jnp.take(direction, cam_index, axis=1)
        return to_cameras(schur_obs(cam_jac, lm_jac, inverse, cam_values), cam_index, CAMERAS) + DAMPING * direction

    residual = gradient
    precond = residual / diagonal
    direction = precond
    rz_now = jnp.sum(residual * precond)
    solution = jnp.zeros_like(gradient)
    for iteration in range(ITERS):
        image = product(direction)
        alpha = rz_now / jnp.sum(direction * image)
        solution = solution + alpha * direction
        residual = residual - alpha * image
        if iteration + 1 < ITERS:
            precond = residual / diagonal
            rz_next = jnp.sum(residual * precond)
            direction = precond + (rz_next / rz_now) * direction
            rz_now = rz_next
    cam_obs = camera_apply(cam_jac, jnp.take(solution, cam_index, axis=1))
    landmark_step = land_rhs - apply_inverse(inverse, landmark_side(lm_jac, cam_obs))
    return (solution, residual, landmark_step)
```

```python
import functools

import jax
import jax.numpy as jnp
from jax import lax
from jax.experimental import pallas as pl
from jax.experimental.pallas import tpu as pltpu
from jax.sharding import PartitionSpec as P

DAMPING = 1.0
MESH = pl.DeviceIdType.MESH
F32 = jnp.float32
BF16 = jnp.bfloat16

TILE = 24
K = 8
LM = 512
OBS = K * LM


def split(value):
    high = value.astype(BF16).astype(F32)
    return high, value - high


def rows_sum(value):
    return jnp.sum(value, axis=0, keepdims=True)


def kernel(cj, lj, rs, ci, step_o, res_o, lm_o,
           onehot, tag8, tag16, hot_q, lhs_a, lhs_b, fld_a, fld_b, nat, err, inv, q_sc,
           terms1, terms2, terms3, core1, core2, core3, xy1, xy2, xy3,
           zl1, zl2, zl3, zh1, zh2, zh3, field1, field2, field3, fin,
           s_core, r_core, s_xy, r_xy, s_zl, r_zl, s_zh, r_zh, s_gx, r_gx, s_gc, r_gc, s_fin, r_fin):
    group = lax.axis_index("group")
    dev = lax.axis_index("dev")
    x, c = group // 2, group % 2
    z, y = dev // 4, dev % 4
    xy = x * 4 + y
    zl, zh = z % 4, z // 4

    def at(xx, cc, yy, zz):
        return {"group": xx * 2 + cc, "dev": zz * 4 + yy}

    sibling = at(x, 1 - c, y, z)
    plane = []
    for k in (10, 6, 14, 9, 11, 2, 8, 5, 7, 13, 15, 1, 3, 4, 12):
        xx, yy = (x + k // 4) % 4, (y + k % 4) % 4
        plane.append((xx * 4 + yy, at(xx, c, yy, z)))
    z_low = [((zl + k) % 4, at(x, c, y, zh * 4 + (zl + k) % 4)) for k in (2, 1, 3)]
    z_high = [((zh + k) % 4, at(x, c, y, ((zh + k) % 4) * 4 + zl)) for k in (2, 1, 3)]
    final = []
    for k in (2, 1, 3, 0):
        for o in (1, 0):
            if k or o:
                xx, cc = (x + k) % 4, (c + o) % 2
                final.append((xx * 2 + cc, at(xx, cc, y, z)))

    barrier = pltpu.get_barrier_semaphore()
    others = [sibling] + [d for _, d in plane + z_low + z_high]
    others += [d for (s, d), (k, o) in zip(final, [(k, o) for k in (2, 1, 3, 0) for o in (1, 0) if k or o]) if k and o]
    for d in others:
        pl.semaphore_signal(barrier, inc=1, device_id=d, device_id_type=MESH)

    iota256 = lax.broadcasted_iota(jnp.int32, (256, LM), 0)
    iota32 = lax.broadcasted_iota(jnp.int32, (32, LM), 0)
    for k in range(K):
        ks = pl.ds(k * LM, LM)
        cam = ci[k:k + 1, :]
        low = (cam >> 9) * 16 + (cam & 15)
        tag = ((cam >> 4) & 1) * 16 + ((cam >> 5) & 3) * 4 + ((cam >> 7) & 3)
        onehot[:, ks] = jnp.where(iota256 == low, 1.0, 0.0).astype(BF16)
        hot_q[:, ks] = jnp.where(iota32 == tag, 1.0, 0.0).astype(BF16)
        tag8[:, ks] = jnp.broadcast_to(tag, (8, LM))
        tag16[:, ks] = jnp.broadcast_to(tag.astype(F32), (16, LM)).astype(BF16)

    def put_terms(base_a, base_b, k, first8, last):
        ks = pl.ds(k * LM, LM)
        both = jnp.concatenate(split(first8), axis=0).astype(BF16)
        tags = tag16[:, ks]
        for q in range(32):
            lhs_a[base_a + q * 16:base_a + q * 16 + 16, ks] = jnp.where(tags == BF16(q), both, BF16(0))
        high, low = split(last)
        hot = hot_q[:, ks]
        lhs_b[base_b:base_b + 32, ks] = hot * jnp.broadcast_to(high, (32, LM)).astype(BF16)
        lhs_b[base_b + 32:base_b + 64, ks] = hot * jnp.broadcast_to(low, (32, LM)).astype(BF16)

    def dot_t(left, right):
        return lax.dot_general(left, right, (((1,), (1,)), ((), ())), preferred_element_type=F32)

    iota_rows = lax.broadcasted_iota(jnp.int32, (8, 128), 0)

    def scatter(terms, base_a, base_b, row, scalar):
        out_a = dot_t(lhs_a[base_a:base_a + 512, :], onehot[...])
        out_b = dot_t(lhs_b[base_b:base_b + 64, :], onehot[...])
        last = out_b[0:32] + out_b[32:64]
        for q in range(32):
            both = out_a[q * 16:q * 16 + 8] + out_a[q * 16 + 8:q * 16 + 16]
            terms[q // 16, q % 16, row:row + 8, :] = both[:, 0:128]
            terms[q // 16, q % 16, row + 8:row + 16, :] = both[:, 128:256]
            terms[q // 16, q % 16, row + 16:row + 24, :] = jnp.where(
                iota_rows == 0, last[q:q + 1, 0:128], jnp.where(
                    iota_rows == 1, last[q:q + 1, 128:256], jnp.where(iota_rows == 2, scalar, 0.0)))

    def push(src, dst, send, recv, device):
        copy = pltpu.make_async_remote_copy(
            src_ref=src, dst_ref=dst, send_sem=send, recv_sem=recv, device_id=device, device_id_type=MESH)
        copy.start()
        return copy

    def landed(dst, sem):
        pltpu.make_async_copy(dst, dst, sem).wait()

    def total(buf, count):
        out = buf[0]
        for k in range(1, count):
            out = out + buf[k]
        return out

    def exchange(n, source, own, mine, partners, buf, s_sem, r_sem, copies):
        for i, (slot, device) in enumerate(partners):
            copies.append(push(source(slot), buf.at[mine], s_sem.at[n, i], r_sem.at[n, mine], device))
        if own is not None:
            buf[mine] = own
        for slot, _ in partners:
            landed(buf.at[slot], r_sem.at[n, slot])

    def reduce(n, terms, core_buf, xy_buf, zl_buf, zh_buf, copies):
        copy = push(terms.at[1 - c], core_buf, s_core.at[n], r_core.at[n], sibling)
        copies.append(copy)
        landed(core_buf, r_core.at[n])
        terms[c] = terms[c] + core_buf[...]
        exchange(n, lambda s: terms.at[c, s], terms[c, xy], xy, plane, xy_buf, s_xy, r_xy, copies)
        zl_buf[zl] = total(xy_buf, 16)
        exchange(n, lambda s: zl_buf.at[zl], None, zl, z_low, zl_buf, s_zl, r_zl, copies)
        zh_buf[zh] = total(zl_buf, 4)
        exchange(n, lambda s: zh_buf.at[zh], None, zh, z_high, zh_buf, s_zh, r_zh, copies)
        return total(zh_buf, 4)

    def gather(n, tile, field, copies):
        field[c, xy] = tile
        for i, (slot, device) in enumerate(plane):
            copies.append(push(field.at[c, xy], field.at[c, xy], s_gx.at[n, i], r_gx.at[n, xy], device))
        for slot, _ in plane:
            landed(field.at[c, slot], r_gx.at[n, slot])
        copies.append(push(field.at[c], field.at[c], s_gc.at[n], r_gc.at[n], sibling))
        landed(field.at[1 - c], r_gc.at[n])

    def entry(first, second):
        return rows_sum(lj[0, first] * lj[0, second] + lj[1, first] * lj[1, second])

    w_00 = entry(0, 0) + DAMPING
    w_11 = entry(1, 1) + DAMPING
    w_22 = entry(2, 2) + DAMPING
    w_01 = entry(0, 1)
    w_02 = entry(0, 2)
    w_12 = entry(1, 2)
    cof_00 = w_11 * w_22 - w_12 * w_12
    cof_01 = w_02 * w_12 - w_01 * w_22
    cof_02 = w_01 * w_12 - w_02 * w_11
    cof_11 = w_00 * w_22 - w_02 * w_02
    cof_12 = w_01 * w_02 - w_00 * w_12
    cof_22 = w_00 * w_11 - w_01 * w_01
    determinant = w_00 * cof_00 + w_01 * cof_01 + w_02 * cof_02
    for i, cof in enumerate((cof_00, cof_01, cof_02, cof_11, cof_12, cof_22)):
        inv[i:i + 1, :] = cof / determinant

    def eliminate(a0, a1, where):
        side = [rows_sum(lj[0, j] * a0 + lj[1, j] * a1) for j in range(3)]
        picks = ((0, 1, 2), (1, 3, 4), (2, 4, 5))
        e0, e1 = a0, a1
        for j in range(3):
            q = sum(inv[p:p + 1, :] * side[m] for m, p in enumerate(picks[j]))
            q_sc[where * 3 + j:where * 3 + j + 1, :] = q
            e0 = e0 - lj[0, j] * q
            e1 = e1 - lj[1, j] * q
        err[0] = e0
        err[1] = e1
        return e0, e1

    def cam_rows(i, k):
        return cj[i, 0:8, k, :]

    copies = []

    e0, e1 = eliminate(rs[0], rs[1], 0)
    grad_last = cj[0, 8] * e0 + cj[1, 8] * e1
    diag_last = cj[0, 8] * cj[0, 8] + cj[1, 8] * cj[1, 8]
    nat[0] = grad_last
    nat[1] = diag_last
    for k in range(K):
        c0, c1 = cam_rows(0, k), cam_rows(1, k)
        put_terms(0, 0, k, c0 * err[0, k:k + 1, :] + c1 * err[1, k:k + 1, :], nat[0, k:k + 1, :])
        put_terms(512, 64, k, c0 * c0 + c1 * c1, nat[1, k:k + 1, :])
    zero = jnp.zeros((1, 128), F32)
    scatter(terms1, 0, 0, 0, zero)
    scatter(terms1, 512, 64, TILE, zero)

    pl.semaphore_wait(barrier, len(others))

    summed = reduce(0, terms1, core1, xy1, zl1, zh1, copies)
    iota_tile = lax.broadcasted_iota(jnp.int32, (TILE, 128), 0)
    real = iota_tile < 18

    def inner(left, right):
        return jnp.sum(jnp.where(real, left * right, 0.0), keepdims=True)

    residual = jnp.where(real, summed[0:TILE], 0.0)
    diagonal = jnp.where(real, summed[TILE:2 * TILE], 0.0) + DAMPING
    precond = residual / diagonal
    gather(0, jnp.where(iota_tile == 18, inner(residual, precond), precond), field1, copies)

    def rz_total(field):
        out = field[0, 0, 18:19, :]
        for q in range(1, 32):
            out = out + field[q // 16, q % 16, 18:19, :]
        return out

    def load_field(field):
        square = jnp.zeros((8, 128), F32)
        for q in range(32):
            part = field[q // 16, q % 16]
            h0, l0 = split(part[0:8])
            h1, l1 = split(part[8:16])
            fld_a[q * 16:q * 16 + 16, 0:128] = jnp.concatenate([h0, l0], axis=0).astype(BF16)
            fld_a[q * 16:q * 16 + 16, 128:256] = jnp.concatenate([h1, l1], axis=0).astype(BF16)
            square = square + part[0:8] * part[0:8] + part[8:16] * part[8:16]
        for half in range(2):
            last = jnp.concatenate([field[0, :, 16 + half, :], field[1, :, 16 + half, :]], axis=0)
            high, low = split(last)
            fld_b[0:32, half * 128:half * 128 + 128] = high.astype(BF16)
            fld_b[32:64, half * 128:half * 128 + 128] = low.astype(BF16)
            for s in range(4):
                square = square + last[s * 8:s * 8 + 8] * last[s * 8:s * 8 + 8]
        return jnp.sum(square, keepdims=True)

    def apply(field, where, terms):
        square = load_field(field)
        for k in range(K):
            ks = pl.ds(k * LM, LM)
            out_a = jnp.dot(fld_a[...], onehot[:, ks], preferred_element_type=F32)
            out_b = jnp.dot(fld_b[...], onehot[:, ks], preferred_element_type=F32)
            tags = tag8[:, ks]
            high, low = out_a[0:8], out_a[8:16]
            for q in range(1, 32):
                hit = tags == q
                high = jnp.where(hit, out_a[q * 16:q * 16 + 8], high)
                low = jnp.where(hit, out_a[q * 16 + 8:q * 16 + 16], low)
            values = high + low
            last = rows_sum((out_b[0:32] + out_b[32:64]) * hot_q[:, ks].astype(F32))
            for i in range(2):
                nat[i, k:k + 1, :] = rows_sum(cam_rows(i, k) * values)
            nat[2, k:k + 1, :] = last
        a0 = nat[0] + cj[0, 8] * nat[2]
        a1 = nat[1] + cj[1, 8] * nat[2]
        e0, e1 = eliminate(a0, a1, where)
        nat[0] = cj[0, 8] * e0 + cj[1, 8] * e1
        product = jnp.sum(a0 * e0 + a1 * e1, keepdims=True)
        for k in range(K):
            put_terms(0, 0, k, cam_rows(0, k) * err[0, k:k + 1, :] + cam_rows(1, k) * err[1, k:k + 1, :], nat[0, k:k + 1, :])
        scatter(terms, 0, 0, 0, jnp.broadcast_to(product, (1, 128)))
        return square

    rz = rz_total(field1)
    square = apply(field1, 1, terms2)
    image = reduce(1, terms2, core2, xy2, zl2, zh2, copies)
    direction = jnp.where(real, field1[c, xy], 0.0)
    alpha1 = rz / (image[18:19] + DAMPING * square)
    residual = residual - alpha1 * jnp.where(real, image + DAMPING * direction, 0.0)
    precond = residual / diagonal
    gather(1, jnp.where(iota_tile == 18, inner(residual, precond), precond), field2, copies)

    rz_next = rz_total(field2)
    beta = rz_next / rz
    for h in range(2):
        for q in range(16):
            field3[h, q] = field2[h, q] + beta * field1[h, q]
    square = apply(field3, 2, terms3)
    image = reduce(2, terms3, core3, xy3, zl3, zh3, copies)
    direction2 = jnp.where(real, field3[c, xy], 0.0)
    alpha2 = rz_next / (image[18:19] + DAMPING * square)
    residual = residual - alpha2 * jnp.where(real, image + DAMPING * direction2, 0.0)
    step = alpha1 * direction + alpha2 * direction2

    low_half = z < 8
    pieces = jnp.concatenate([
        jnp.where(low_half, step[0:8], step[8:16]),
        jnp.where(low_half, residual[0:8], residual[8:16]),
        jnp.where(iota_rows == 0, jnp.where(low_half, step[16:17], step[17:18]),
                  jnp.where(iota_rows == 1, jnp.where(low_half, residual[16:17], residual[17:18]), 0.0)),
    ], axis=0)
    moved = pltpu.roll(pieces, (group * 16 - (z % 8) * 16 + 128) % 128, 1)
    lane = lax.broadcasted_iota(jnp.int32, (TILE, 128), 1)
    fin[group] = jnp.where(lane // 16 == group, moved, 0.0)
    for i, (slot, device) in enumerate(final):
        copies.append(push(fin.at[group], fin.at[group], s_fin.at[i], r_fin.at[group], device))

    scale1 = jnp.concatenate([alpha1] * 4, axis=1)
    scale2 = jnp.concatenate([alpha2] * 4, axis=1)
    lm_o[...] = q_sc[0:3, :] - scale1 * q_sc[3:6, :] - scale2 * q_sc[6:9, :]

    for slot, _ in final:
        landed(fin.at[slot], r_fin.at[slot])
    whole = total(fin, 8)
    step_o[0:8, :] = whole[0:8]
    step_o[8:9, :] = whole[16:17]
    res_o[0:8, :] = whole[8:16]
    res_o[8:9, :] = whole[17:18]
    for copy in copies:
        copy.wait_send()


def body(cam_jac, lm_jac, resid, cam_index):
    vmem = pl.BlockSpec(memory_space=pltpu.VMEM)

    def tiles(*lead):
        return pltpu.VMEM(lead + (TILE, 128), F32)

    def wide(*lead):
        return pltpu.VMEM(lead + (2 * TILE, 128), F32)

    dma = pltpu.SemaphoreType.DMA
    scratch = [
        pltpu.VMEM((256, OBS), BF16), pltpu.VMEM((8, OBS), jnp.int32), pltpu.VMEM((16, OBS), BF16), pltpu.VMEM((32, OBS), BF16),
        pltpu.VMEM((1024, OBS), BF16), pltpu.VMEM((128, OBS), BF16), pltpu.VMEM((512, 256), BF16), pltpu.VMEM((64, 256), BF16),
        pltpu.VMEM((3, K, LM), F32), pltpu.VMEM((2, K, LM), F32), pltpu.VMEM((8, LM), F32), pltpu.VMEM((16, LM), F32),
        wide(2, 16), tiles(2, 16), tiles(2, 16), wide(16), tiles(16), tiles(16), wide(16), tiles(16), tiles(16),
        wide(4), tiles(4), tiles(4), wide(4), tiles(4), tiles(4), tiles(2, 16), tiles(2, 16), tiles(2, 16), tiles(8),
        dma((3,)), dma((3,)), dma((3, 15)), dma((3, 16)), dma((3, 3)), dma((3, 4)), dma((3, 3)), dma((3, 4)),
        dma((2, 15)), dma((2, 16)), dma((2,)), dma((2,)), dma((7,)), dma((8,)),
    ]
    return pl.pallas_call(
        kernel,
        out_shape=(jax.ShapeDtypeStruct((9, 128), F32), jax.ShapeDtypeStruct((9, 128), F32), jax.ShapeDtypeStruct((3, LM), F32)),
        in_specs=[vmem] * 4,
        out_specs=(vmem, vmem, vmem),
        scratch_shapes=scratch,
        name="schur_cg",
        compiler_params=pltpu.CompilerParams(collective_id=0, has_side_effects=True, vmem_limit_bytes=56 << 20),
    )(cam_jac, lm_jac, resid, cam_index)


def solution(mesh):
    in_specs = (
        P(None, None, None, ("group", "dev")),
        P(None, None, None, ("group", "dev")),
        P(None, None, ("group", "dev")),
        P(None, ("group", "dev")),
    )
    out_specs = (P(None, "dev"), P(None, "dev"), P(None, ("group", "dev")))
    return jax.shard_map(body, mesh=mesh, in_specs=in_specs, out_specs=out_specs, check_vma=False)
```

```python
import functools

import jax
import jax.numpy as jnp
from jax import lax
from jax.experimental import pallas as pl
from jax.experimental.pallas import tpu as pltpu
from jax.sharding import PartitionSpec as P

DAMPING = 1.0
MESH = pl.DeviceIdType.MESH
F32 = jnp.float32
BF16 = jnp.bfloat16

TILE = 20
K = 8
LM = 512
OBS = K * LM
FLOWS = 4


def split(value):
    high = value.astype(BF16).astype(F32)
    return high, value - high


def rows_sum(value):
    return jnp.sum(value, axis=0, keepdims=True)


def total(buf, count):
    out = buf[0]
    for k in range(1, count):
        out = out + buf[k]
    return out


def kernel(cj_hbm, lj_hbm, rs_hbm, ci_hbm, step_o, res_o, lm_o,
           cj, lj, rs, ci, onehot, tag8, tag16, hot_q, both_sc, last_sc, lhs, fld, acc, last_acc, nat, first_a, err, inv, q_sc,
           terms, cores, plane_buf, pair_buf, even_buf, z_buf, slice_out, slice_in, fields, packed, fin,
           s_core, r_core, s_xy, r_xy, s_zp, r_zp, s_ze, r_ze, s_z, r_z, s_gx, r_gx, s_gc, r_gc, s_fin, r_fin, s_in):
    group = lax.axis_index("group")
    dev = lax.axis_index("dev")
    x, c = group // 2, group % 2
    z, y = dev // 4, dev % 4
    xy = x * 4 + y

    def at(xx, cc, yy, zz):
        return {"group": xx * 2 + cc, "dev": zz * 4 + yy}

    sibling = at(x, 1 - c, y, z)
    plane = []
    for k in (10, 6, 14, 9, 11, 2, 8, 5, 7, 13, 15, 1, 3, 4, 12):
        xx, yy = (x + k // 4) % 4, (y + k % 4) % 4
        plane.append((xx * 4 + yy, at(xx, c, yy, z)))
    pair = z // 2 * 2 + 1 - z % 2
    column = [((z + k) % 16, at(x, c, y, (z + k) % 16)) for k in (8, 7, 9, 6, 10, 5, 11, 4, 12, 3, 13, 2, 14, 1, 15)]
    evens = [((z + k) % 16 // 2, at(x, c, y, (z + k) % 16)) for k in (8, 6, 10, 4, 12, 2, 14)]
    family, cousins = [], []
    for k in (2, 1, 3, 0):
        for o in (1, 0):
            if k or o:
                xx, cc = (x + k) % 4, (c + o) % 2
                family.append((xx * 2 + cc, at(xx, cc, y, z)))
                if k and o:
                    cousins.append(at(xx, cc, y, z))

    barrier = pltpu.get_barrier_semaphore()
    others = [d for _, d in column + plane] + cousins + [sibling]
    for d in others:
        pl.semaphore_signal(barrier, inc=1, device_id=d, device_id_type=MESH)

    loads = [pltpu.make_async_copy(a, b, s_in.at[i])
             for i, (a, b) in enumerate(((ci_hbm, ci), (lj_hbm, lj), (rs_hbm, rs), (cj_hbm, cj)))]
    for load in loads:
        load.start()
    loads[0].wait()

    iota256 = lax.broadcasted_iota(jnp.int32, (256, LM), 0)
    iota32 = lax.broadcasted_iota(jnp.int32, (32, LM), 0)
    for k in range(K):
        ks = pl.ds(k * LM, LM)
        cam = ci[k:k + 1, :]
        low = (cam >> 9) * 16 + (cam & 15)
        tag = (((cam >> 4) & 1) ^ c) * 16 + ((cam >> 5) & 3) * 4 + ((cam >> 7) & 3)
        onehot[:, ks] = jnp.where(iota256 == low, 1.0, 0.0).astype(BF16)
        hot_q[:, ks] = jnp.where(iota32 == tag, 1.0, 0.0).astype(BF16)
        tag8[:, ks] = jnp.broadcast_to(tag, (8, LM))
        tag16[:, ks] = jnp.broadcast_to(tag.astype(F32), (16, LM)).astype(BF16)

    def prepare(k, first8, last):
        ks = pl.ds(k * LM, LM)
        both_sc[:, ks] = jnp.concatenate(split(first8), axis=0).astype(BF16)
        high, low = split(last)
        last_sc[0:1, ks] = high
        last_sc[1:2, ks] = low

    def put_half(base, h):
        for k in range(K):
            ks = pl.ds(k * LM, LM)
            both = both_sc[:, ks]
            tags = tag16[:, ks]
            row = base + h * 288
            for q in range(16):
                lhs[row + q * 16:row + q * 16 + 16, ks] = jnp.where(tags == BF16(h * 16 + q), both, BF16(0))
            hot = hot_q[h * 16:h * 16 + 16, ks]
            lhs[row + 256:row + 272, ks] = hot * jnp.broadcast_to(last_sc[0:1, ks], (16, LM)).astype(BF16)
            lhs[row + 272:row + 288, ks] = hot * jnp.broadcast_to(last_sc[1:2, ks], (16, LM)).astype(BF16)

    def dot_t(left, right):
        return lax.dot_general(left, right, (((1,), (1,)), ((), ())), preferred_element_type=F32)

    iota_rows = lax.broadcasted_iota(jnp.int32, (8, 128), 0)
    lane = lax.broadcasted_iota(jnp.int32, (8, 128), 1)

    def scatter_half(n, base, h, scalar):
        put_half(base, h)
        out = dot_t(lhs[base + h * 288:base + h * 288 + 288, :], onehot[...])
        last = out[256:272] + out[272:288]
        for q in range(16):
            both = out[q * 16:q * 16 + 8] + out[q * 16 + 8:q * 16 + 16]
            terms[n, h, q, 0:8, :] = both[:, 0:128]
            terms[n, h, q, 8:16, :] = both[:, 128:256]
            tail = jnp.where(
                iota_rows == 0, last[q:q + 1, 0:128], jnp.where(
                    iota_rows == 1, last[q:q + 1, 128:256], jnp.where(iota_rows == 2, scalar, 0.0)))
            terms[n, h, q, 16:20, :] = tail[0:4]

    copies = []

    def push(src, dst, send, recv, device):
        copy = pltpu.make_async_remote_copy(
            src_ref=src, dst_ref=dst, send_sem=send, recv_sem=recv, device_id=device, device_id_type=MESH)
        copy.start()
        copies.append(copy)

    def drain(keep):
        while len(copies) > keep:
            copies.pop(0).wait_send()

    def landed(dst, sem):
        pltpu.make_async_copy(dst, dst, sem).wait()

    def start_core(n):
        for i, slot in enumerate([s for s, _ in plane] + [xy]):
            push(terms.at[n, 1, slot], cores.at[n, slot], s_core.at[n, i], r_core.at[n, slot], sibling)

    def start_plane(n):
        for i, (slot, device) in enumerate(plane):
            landed(cores.at[n, slot], r_core.at[n, slot])
            terms[n, 0, slot] = terms[n, 0, slot] + cores[n, slot]
            push(terms.at[n, 0, slot], plane_buf.at[n, xy], s_xy.at[n, i], r_xy.at[n, xy], device)
        landed(cores.at[n, xy], r_core.at[n, xy])
        plane_buf[n, xy] = terms[n, 0, xy] + cores[n, xy]

    def end_plane(n):
        for slot, _ in plane[::-1]:
            landed(plane_buf.at[n, slot], r_xy.at[n, slot])
        return total(plane_buf.at[n], 16)

    def start_gather(n, tile):
        fields[n, 0, xy] = tile
        for i, (slot, device) in enumerate(plane):
            push(fields.at[n, 0, xy], fields.at[n, 0, xy], s_gx.at[n, i], r_gx.at[n, xy], device)
        push(fields.at[n, 0, xy], fields.at[n, 1, xy], s_gc.at[n, 15], r_gc.at[n, xy], sibling)
        for i, (slot, _) in enumerate(plane[::-1]):
            landed(fields.at[n, 0, slot], r_gx.at[n, slot])
            push(fields.at[n, 0, slot], fields.at[n, 1, slot], s_gc.at[n, i], r_gc.at[n, slot], sibling)

    def end_gather(n):
        for slot in [xy] + [s for s, _ in plane[::-1]]:
            landed(fields.at[n, 1, slot], r_gc.at[n, slot])

    def entry(first, second):
        return rows_sum(lj[0, first] * lj[0, second] + lj[1, first] * lj[1, second])

    loads[1].wait()
    loads[2].wait()
    loads[3].wait()
    w_00 = entry(0, 0) + DAMPING
    w_11 = entry(1, 1) + DAMPING
    w_22 = entry(2, 2) + DAMPING
    w_01 = entry(0, 1)
    w_02 = entry(0, 2)
    w_12 = entry(1, 2)
    cof_00 = w_11 * w_22 - w_12 * w_12
    cof_01 = w_02 * w_12 - w_01 * w_22
    cof_02 = w_01 * w_12 - w_02 * w_11
    cof_11 = w_00 * w_22 - w_02 * w_02
    cof_12 = w_01 * w_02 - w_00 * w_12
    cof_22 = w_00 * w_11 - w_01 * w_01
    determinant = w_00 * cof_00 + w_01 * cof_01 + w_02 * cof_02
    for i, cof in enumerate((cof_00, cof_01, cof_02, cof_11, cof_12, cof_22)):
        inv[i:i + 1, :] = cof / determinant

    def eliminate(a0, a1, where):
        side = [rows_sum(lj[0, j] * a0 + lj[1, j] * a1) for j in range(3)]
        picks = ((0, 1, 2), (1, 3, 4), (2, 4, 5))
        e0, e1 = a0, a1
        for j in range(3):
            q = sum(inv[p:p + 1, :] * side[m] for m, p in enumerate(picks[j]))
            q_sc[where * 3 + j:where * 3 + j + 1, :] = q
            e0 = e0 - lj[0, j] * q
            e1 = e1 - lj[1, j] * q
        err[0] = e0
        err[1] = e1
        return e0, e1

    def cam_rows(i, k):
        return cj[i, 0:8, k, :]

    zero = jnp.zeros((1, 128), F32)
    e0, e1 = eliminate(rs[0], rs[1], 0)
    nat[0] = cj[0, 8] * e0 + cj[1, 8] * e1
    nat[1] = cj[0, 8] * cj[0, 8] + cj[1, 8] * cj[1, 8]
    for k in range(K):
        prepare(k, cam_rows(0, k) * err[0, k:k + 1, :] + cam_rows(1, k) * err[1, k:k + 1, :], nat[0, k:k + 1, :])
    scatter_half(0, 0, 1, zero)
    pl.semaphore_wait(barrier, len(others))
    start_core(0)
    scatter_half(0, 0, 0, zero)
    for k in range(K):
        c0, c1 = cam_rows(0, k), cam_rows(1, k)
        prepare(k, c0 * c0 + c1 * c1, nat[1, k:k + 1, :])
    scatter_half(1, 576, 1, zero)
    start_core(1)
    start_plane(0)
    scatter_half(1, 576, 0, zero)
    start_plane(1)

    for n in range(2):
        pair_buf[n, z % 2] = end_plane(n)
        push(pair_buf.at[n, z % 2], pair_buf.at[n, z % 2], s_zp.at[n], r_zp.at[n, z % 2], at(x, c, y, pair))
    for n in range(2):
        landed(pair_buf.at[n, pair % 2], r_zp.at[n, pair % 2])
        even_buf[n, z // 2] = total(pair_buf.at[n], 2)
        for i, (slot, device) in enumerate(evens):
            push(even_buf.at[n, z // 2], even_buf.at[n, z // 2], s_ze.at[n, i], r_ze.at[n, z // 2], device)
    drain(2 * len(evens))
    for n in range(2):
        for slot, _ in evens:
            landed(even_buf.at[n, slot], r_ze.at[n, slot])
    summed = [total(even_buf.at[n], 8) for n in range(2)]
    real = lax.broadcasted_iota(jnp.int32, (TILE, 128), 0) < 18
    scalar_row = lax.broadcasted_iota(jnp.int32, (TILE, 128), 0) == 18

    def inner(left, right):
        return jnp.sum(jnp.where(real, left * right, 0.0), keepdims=True)

    residual = jnp.where(real, summed[0], 0.0)
    diagonal = jnp.where(real, summed[1], 0.0) + DAMPING
    precond = residual / diagonal

    def rz_half(n, h):
        out = fields[n, h, 0, 18:19, :]
        for s in range(1, 16):
            out = out + fields[n, h, s, 18:19, :]
        return out

    def load_half(n, h):
        for s in range(16):
            part = fields[n, h, s]
            h0, l0 = split(part[0:8])
            h1, l1 = split(part[8:16])
            row = h * 288 + s * 16
            fld[row:row + 16, 0:128] = jnp.concatenate([h0, l0], axis=0).astype(BF16)
            fld[row:row + 16, 128:256] = jnp.concatenate([h1, l1], axis=0).astype(BF16)
        for b in range(2):
            high, low = split(fields[n, h, :, 16 + b, :])
            fld[h * 288 + 256:h * 288 + 272, b * 128:b * 128 + 128] = high.astype(BF16)
            fld[h * 288 + 272:h * 288 + 288, b * 128:b * 128 + 128] = low.astype(BF16)

    def pick_half(h, k):
        ks = pl.ds(k * LM, LM)
        out = jnp.dot(fld[h * 288:h * 288 + 288, :], onehot[:, ks], preferred_element_type=F32)
        tags = tag8[:, ks]
        if h:
            high, low = acc[0:8, ks], acc[8:16, ks]
        else:
            high, low = jnp.zeros((8, LM), F32), jnp.zeros((8, LM), F32)
        for s in range(16):
            hit = tags == h * 16 + s
            high = jnp.where(hit, out[s * 16:s * 16 + 8], high)
            low = jnp.where(hit, out[s * 16 + 8:s * 16 + 16], low)
        last = (out[256:272] + out[272:288]) * hot_q[h * 16:h * 16 + 16, ks].astype(F32)
        return high, low, last[0:8] + last[8:16]

    def apply(n, where, wait, flow):
        load_half(n, 0)
        for k in range(K):
            ks = pl.ds(k * LM, LM)
            high, low, last = pick_half(0, k)
            acc[0:8, ks] = high
            acc[8:16, ks] = low
            last_acc[:, ks] = last
        wait()
        load_half(n, 1)
        for k in range(K):
            high, low, last = pick_half(1, k)
            values = high + low
            for i in range(2):
                nat[i, k:k + 1, :] = rows_sum(cam_rows(i, k) * values)
            nat[2, k:k + 1, :] = rows_sum(last + last_acc[:, pl.ds(k * LM, LM)])
        a0 = nat[0] + cj[0, 8] * nat[2]
        a1 = nat[1] + cj[1, 8] * nat[2]
        if n:
            beta = jnp.concatenate([(rz_half(1, 0) + rz_half(1, 1)) / (rz_half(0, 0) + rz_half(0, 1))] * 4, axis=1)
            a0 = a0 + beta * first_a[0]
            a1 = a1 + beta * first_a[1]
        else:
            first_a[0] = a0
            first_a[1] = a1
        e0, e1 = eliminate(a0, a1, where)
        nat[0] = cj[0, 8] * e0 + cj[1, 8] * e1
        product = jnp.sum(a0 * e0 + a1 * e1, keepdims=True)
        for k in range(K):
            prepare(k, cam_rows(0, k) * err[0, k:k + 1, :] + cam_rows(1, k) * err[1, k:k + 1, :], nat[0, k:k + 1, :])
        product = jnp.broadcast_to(product, (1, 128))
        scatter_half(flow, 0, 1, product)
        start_core(flow)
        scatter_half(flow, 0, 0, product)
        start_plane(flow)

    start_gather(0, jnp.where(scalar_row, inner(residual, precond), precond))
    apply(0, 1, lambda: end_gather(0), 2)
    rz = rz_half(0, 0) + rz_half(0, 1)

    def square_half(h, scale):
        out = jnp.zeros((TILE, 128), F32)
        for s in range(16):
            part = fields[0, h, s] if scale is None else fields[1, h, s] + scale * fields[0, h, s]
            out = out + part * part
        return jnp.sum(jnp.where(real, out, 0.0), keepdims=True)

    square = square_half(0, None) + square_half(1, None)
    z_buf[z] = end_plane(2)
    for i, (slot, device) in enumerate(column):
        push(z_buf.at[z], z_buf.at[z], s_z.at[0, i], r_z.at[0, z], device)
    drain(len(column))
    direction = jnp.where(real, fields[0, 0, xy], 0.0)
    for slot, _ in column:
        landed(z_buf.at[slot], r_z.at[0, slot])
    image = total(z_buf, 16)
    alpha1 = rz / (image[18:19] + DAMPING * square)
    residual = residual - alpha1 * jnp.where(real, image + DAMPING * direction, 0.0)
    precond = residual / diagonal
    start_gather(1, jnp.where(scalar_row, inner(residual, precond), precond))

    apply(1, 2, lambda: end_gather(1), 3)
    rz_next = rz_half(1, 0) + rz_half(1, 1)
    beta = rz_next / rz

    square = square_half(0, beta) + square_half(1, beta)

    def swap(value):
        out = value
        for d in range(1, 8):
            moved = pltpu.roll(pltpu.roll(value, 16 * d, 1), 8 - d, 0)
            out = jnp.where((lane // 16 - iota_rows + 8) % 8 == d, moved, out)
        return out

    def pack(store, tile, scalar):
        for b in range(2):
            first = swap(tile[b * 8:b * 8 + 8])
            row = jnp.broadcast_to(tile[16 + b:17 + b], (8, 128))
            second = row
            for g in range(1, 8):
                second = jnp.where(iota_rows == g, pltpu.roll(row, 128 - 16 * g, 1), second)
            second = jnp.where(lane < 16, second, scalar)
            for g in range(8):
                store[b * 8 + g, 0:1, :] = first[g:g + 1]
                store[b * 8 + g, 1:2, :] = second[g:g + 1]

    direction2 = jnp.where(real, fields[1, 0, xy] + beta * direction, 0.0)
    for i, tile in enumerate((direction, direction2, residual)):
        pack(packed.at[i], tile, 0.0)

    own = end_plane(3)
    pack(slice_out, own, jnp.broadcast_to(own[18:19], (8, 128)))
    for i, (slot, device) in enumerate(column):
        push(slice_out.at[slot], slice_in.at[z], s_z.at[1, i], r_z.at[1, z], device)
    slice_in[z] = slice_out[z]
    drain(len(column))
    for slot, _ in column:
        landed(slice_in.at[slot], r_z.at[1, slot])
    image = total(slice_in, 16)
    pick = lax.broadcasted_iota(jnp.int32, (2, 128), 0) * 128 + lax.broadcasted_iota(jnp.int32, (2, 128), 1)
    product = jnp.sum(jnp.where(pick == 144, image, 0.0), keepdims=True)
    alpha2 = rz_next / (product + DAMPING * square)
    fin[group, 0:2, :] = alpha1 * packed[0, z] + alpha2 * packed[1, z]
    fin[group, 2:4, :] = packed[2, z] - alpha2 * (image + DAMPING * packed[1, z])

    for i, (slot, device) in enumerate(family):
        push(fin.at[group], fin.at[group], s_fin.at[i], r_fin.at[group], device)

    scale1 = jnp.concatenate([alpha1] * 4, axis=1)
    scale2 = jnp.concatenate([alpha2] * 4, axis=1)
    lm_o[...] = q_sc[0:3, :] - scale1 * q_sc[3:6, :] - scale2 * q_sc[6:9, :]
    drain(len(family))

    for slot, _ in family:
        landed(fin.at[slot], r_fin.at[slot])
    for i, out in enumerate((step_o, res_o)):
        out[0:8, :] = swap(fin[:, 2 * i, :])
        second = fin[:, 2 * i + 1, :]
        row = second[0:1]
        for g in range(1, 8):
            row = jnp.where(lane[0:1] // 16 == g, pltpu.roll(second, 16 * g, 1)[g:g + 1], row)
        out[8:9, :] = row
    drain(0)


def deliver(step, res, lm, step_o, res_o, lm_o):
    step_o[...] = step[...]
    res_o[...] = res[...]
    lm_o[...] = lm[...]


def body(cam_jac, lm_jac, resid, cam_index):
    vmem = pl.BlockSpec(memory_space=pltpu.VMEM)

    def tiles(*lead):
        return pltpu.VMEM(lead + (TILE, 128), F32)

    dma = pltpu.SemaphoreType.DMA
    scratch = [
        pltpu.VMEM((2, 9, K, LM), F32), pltpu.VMEM((2, 3, K, LM), F32), pltpu.VMEM((2, K, LM), F32), pltpu.VMEM((K, LM), jnp.int32),
        pltpu.VMEM((256, OBS), BF16), pltpu.VMEM((8, OBS), jnp.int32), pltpu.VMEM((16, OBS), BF16), pltpu.VMEM((32, OBS), BF16),
        pltpu.VMEM((16, OBS), BF16), pltpu.VMEM((2, OBS), F32), pltpu.VMEM((1152, OBS), BF16), pltpu.VMEM((576, 256), BF16),
        pltpu.VMEM((16, OBS), F32), pltpu.VMEM((8, OBS), F32),
        pltpu.VMEM((3, K, LM), F32), pltpu.VMEM((2, K, LM), F32), pltpu.VMEM((2, K, LM), F32), pltpu.VMEM((8, LM), F32), pltpu.VMEM((16, LM), F32),
        tiles(FLOWS, 2, 16), tiles(FLOWS, 16), tiles(FLOWS, 16), tiles(2, 2), tiles(2, 8), tiles(16),
        pltpu.VMEM((16, 2, 128), F32), pltpu.VMEM((16, 2, 128), F32), tiles(2, 2, 16), pltpu.VMEM((3, 16, 2, 128), F32),
        pltpu.VMEM((8, 4, 128), F32),
        dma((FLOWS, 16)), dma((FLOWS, 16)), dma((FLOWS, 15)), dma((FLOWS, 16)), dma((2,)), dma((2, 2)), dma((2, 7)), dma((2, 8)),
        dma((2, 15)), dma((2, 16)), dma((2, 15)), dma((2, 16)), dma((2, 16)), dma((2, 16)), dma((7,)), dma((8,)), dma((4,)),
    ]
    out_shape = (jax.ShapeDtypeStruct((9, 128), F32), jax.ShapeDtypeStruct((9, 128), F32), jax.ShapeDtypeStruct((3, LM), F32))
    results = pl.pallas_call(
        kernel,
        out_shape=out_shape,
        in_specs=[pl.BlockSpec(memory_space=pl.ANY)] * 4,
        out_specs=(vmem, vmem, vmem),
        scratch_shapes=scratch,
        name="schur_cg",
        compiler_params=pltpu.CompilerParams(collective_id=0, has_side_effects=True, vmem_limit_bytes=60 << 20),
    )(cam_jac, lm_jac, resid, cam_index)
    return pl.pallas_call(
        deliver,
        out_shape=out_shape,
        in_specs=[vmem] * 3,
        out_specs=(vmem, vmem, vmem),
        name="deliver",
    )(*results)


def solution(mesh):
    in_specs = (
        P(None, None, None, ("group", "dev")),
        P(None, None, None, ("group", "dev")),
        P(None, None, ("group", "dev")),
        P(None, ("group", "dev")),
    )
    out_specs = (P(None, "dev"), P(None, "dev"), P(None, ("group", "dev")))
    return jax.shard_map(body, mesh=mesh, in_specs=in_specs, out_specs=out_specs, check_vma=False)
```

```python
import functools

import jax
import jax.numpy as jnp
from jax import lax
from jax.experimental import pallas as pl
from jax.experimental.pallas import tpu as pltpu
from jax.sharding import PartitionSpec as P

DAMPING = 1.0
MESH = pl.DeviceIdType.MESH
F32 = jnp.float32
BF16 = jnp.bfloat16

TILE = 20
K = 8
LM = 512
OBS = K * LM
FLOWS = 4


def split(value):
    high = value.astype(BF16).astype(F32)
    return high, value - high


def rows_sum(value):
    return jnp.sum(value, axis=0, keepdims=True)


def total(buf, count):
    out = buf[0]
    for k in range(1, count):
        out = out + buf[k]
    return out


def kernel(cj_hbm, lj_hbm, rs_hbm, ci_hbm, step_o, res_o, lm_o,
           cj, lj, rs, ci, onehot, tag8, tag16, hot_q, both_sc, last_sc, lhs, fld, acc, last_acc, nat, first_a, err, inv, q_sc,
           terms, cores, plane_buf, pair_buf, even_buf, z_buf, slice_out, slice_in, fields, packed, fin,
           s_core, r_core, s_xy, r_xy, s_zp, r_zp, s_ze, r_ze, s_z, r_z, s_gx, r_gx, s_gc, r_gc, s_fin, r_fin, s_in):
    group = lax.axis_index("group")
    dev = lax.axis_index("dev")
    x, c = group // 2, group % 2
    z, y = dev // 4, dev % 4
    xy = x * 4 + y

    def at(xx, cc, yy, zz):
        return {"group": xx * 2 + cc, "dev": zz * 4 + yy}

    sibling = at(x, 1 - c, y, z)
    plane = []
    for k in (10, 6, 14, 9, 11, 2, 8, 5, 7, 13, 15, 1, 3, 4, 12):
        xx, yy = (x + k // 4) % 4, (y + k % 4) % 4
        plane.append((xx * 4 + yy, at(xx, c, yy, z)))
    pair = z // 2 * 2 + 1 - z % 2
    column = [((z + k) % 16, at(x, c, y, (z + k) % 16)) for k in (8, 7, 9, 6, 10, 5, 11, 4, 12, 3, 13, 2, 14, 1, 15)]
    evens = [((z + k) % 16 // 2, at(x, c, y, (z + k) % 16)) for k in (8, 6, 10, 4, 12, 2, 14)]
    family, cousins = [], []
    for k in (2, 1, 3, 0):
        for o in (1, 0):
            if k or o:
                xx, cc = (x + k) % 4, (c + o) % 2
                family.append((xx * 2 + cc, at(xx, cc, y, z)))
                if k and o:
                    cousins.append(at(xx, cc, y, z))

    barrier = pltpu.get_barrier_semaphore()
    others = [d for _, d in column + plane] + cousins + [sibling]
    for d in others:
        pl.semaphore_signal(barrier, inc=1, device_id=d, device_id_type=MESH)

    loads = [pltpu.make_async_copy(a, b, s_in.at[i])
             for i, (a, b) in enumerate(((ci_hbm, ci), (lj_hbm, lj), (rs_hbm, rs), (cj_hbm, cj)))]
    for load in loads:
        load.start()
    loads[0].wait()

    iota256 = lax.broadcasted_iota(jnp.int32, (256, LM), 0)
    iota32 = lax.broadcasted_iota(jnp.int32, (32, LM), 0)
    for k in range(K):
        ks = pl.ds(k * LM, LM)
        cam = ci[k:k + 1, :]
        low = (cam >> 9) * 16 + (cam & 15)
        tag = (((cam >> 4) & 1) ^ c) * 16 + ((cam >> 5) & 3) * 4 + ((cam >> 7) & 3)
        onehot[:, ks] = jnp.where(iota256 == low, 1.0, 0.0).astype(BF16)
        hot_q[:, ks] = jnp.where(iota32 == tag, 1.0, 0.0).astype(BF16)
        tag8[:, ks] = jnp.broadcast_to(tag, (8, LM))
        tag16[:, ks] = jnp.broadcast_to(tag.astype(F32), (16, LM)).astype(BF16)

    def prepare(k, first8, last):
        ks = pl.ds(k * LM, LM)
        both_sc[:, ks] = jnp.concatenate(split(first8), axis=0).astype(BF16)
        high, low = split(last)
        last_sc[0:1, ks] = high
        last_sc[1:2, ks] = low

    def put_half(base, h):
        for k in range(K):
            ks = pl.ds(k * LM, LM)
            both = both_sc[:, ks]
            tags = tag16[:, ks]
            row = base + h * 288
            for q in range(16):
                lhs[row + q * 16:row + q * 16 + 16, ks] = jnp.where(tags == BF16(h * 16 + q), both, BF16(0))
            hot = hot_q[h * 16:h * 16 + 16, ks]
            lhs[row + 256:row + 272, ks] = hot * jnp.broadcast_to(last_sc[0:1, ks], (16, LM)).astype(BF16)
            lhs[row + 272:row + 288, ks] = hot * jnp.broadcast_to(last_sc[1:2, ks], (16, LM)).astype(BF16)

    def dot_t(left, right):
        return lax.dot_general(left, right, (((1,), (1,)), ((), ())), preferred_element_type=F32)

    iota_rows = lax.broadcasted_iota(jnp.int32, (8, 128), 0)
    lane = lax.broadcasted_iota(jnp.int32, (8, 128), 1)

    def scatter_half(n, base, h, scalar):
        put_half(base, h)
        out = dot_t(lhs[base + h * 288:base + h * 288 + 288, :], onehot[...])
        last = out[256:272] + out[272:288]
        for q in range(16):
            both = out[q * 16:q * 16 + 8] + out[q * 16 + 8:q * 16 + 16]
            terms[n, h, q, 0:8, :] = both[:, 0:128]
            terms[n, h, q, 8:16, :] = both[:, 128:256]
            tail = jnp.where(
                iota_rows == 0, last[q:q + 1, 0:128], jnp.where(
                    iota_rows == 1, last[q:q + 1, 128:256], jnp.where(iota_rows == 2, scalar, 0.0)))
            terms[n, h, q, 16:20, :] = tail[0:4]

    pending = []

    def push(src, dst, send, recv, device):
        pltpu.make_async_remote_copy(
            src_ref=src, dst_ref=dst, send_sem=send, recv_sem=recv, device_id=device, device_id_type=MESH).start()

    def landed(dst, sem):
        pltpu.make_async_copy(dst, dst, sem).wait()

    def drain():
        while pending:
            landed(*pending.pop(0))

    def start_core(n):
        push(terms.at[n, 1], cores.at[n], s_core.at[n], r_core.at[n], sibling)
        pending.append((terms.at[n, 1], s_core.at[n]))

    def start_plane(n):
        landed(cores.at[n], r_core.at[n])
        for slot in range(16):
            terms[n, 0, slot] = terms[n, 0, slot] + cores[n, slot]
        for slot, device in plane:
            push(terms.at[n, 0, slot], plane_buf.at[n, xy], s_xy.at[n], r_xy.at[n], device)
        pending.append((plane_buf.at[n, pl.ds(0, 15)], s_xy.at[n]))
        plane_buf[n, xy] = terms[n, 0, xy]

    def end_plane(n):
        landed(plane_buf.at[n, pl.ds(0, 15)], r_xy.at[n])
        return total(plane_buf.at[n], 16)

    def start_gather(n, tile):
        fields[n, 0, xy] = tile
        for slot, device in plane:
            push(fields.at[n, 0, xy], fields.at[n, 0, xy], s_gx.at[n], r_gx.at[n, xy], device)
        pending.append((fields.at[n, 0, pl.ds(0, 15)], s_gx.at[n]))
        push(fields.at[n, 0, xy], fields.at[n, 1, xy], s_gc.at[n], r_gc.at[n], sibling)
        for slot, _ in plane[::-1]:
            landed(fields.at[n, 0, slot], r_gx.at[n, slot])
            push(fields.at[n, 0, slot], fields.at[n, 1, slot], s_gc.at[n], r_gc.at[n], sibling)
        pending.append((fields.at[n, 0], s_gc.at[n]))

    def end_gather(n):
        landed(fields.at[n, 1], r_gc.at[n])

    def entry(first, second):
        return rows_sum(lj[0, first] * lj[0, second] + lj[1, first] * lj[1, second])

    loads[1].wait()
    loads[2].wait()
    loads[3].wait()
    w_00 = entry(0, 0) + DAMPING
    w_11 = entry(1, 1) + DAMPING
    w_22 = entry(2, 2) + DAMPING
    w_01 = entry(0, 1)
    w_02 = entry(0, 2)
    w_12 = entry(1, 2)
    cof_00 = w_11 * w_22 - w_12 * w_12
    cof_01 = w_02 * w_12 - w_01 * w_22
    cof_02 = w_01 * w_12 - w_02 * w_11
    cof_11 = w_00 * w_22 - w_02 * w_02
    cof_12 = w_01 * w_02 - w_00 * w_12
    cof_22 = w_00 * w_11 - w_01 * w_01
    determinant = w_00 * cof_00 + w_01 * cof_01 + w_02 * cof_02
    for i, cof in enumerate((cof_00, cof_01, cof_02, cof_11, cof_12, cof_22)):
        inv[i:i + 1, :] = cof / determinant

    def eliminate(a0, a1, where):
        side = [rows_sum(lj[0, j] * a0 + lj[1, j] * a1) for j in range(3)]
        picks = ((0, 1, 2), (1, 3, 4), (2, 4, 5))
        e0, e1 = a0, a1
        for j in range(3):
            q = sum(inv[p:p + 1, :] * side[m] for m, p in enumerate(picks[j]))
            q_sc[where * 3 + j:where * 3 + j + 1, :] = q
            e0 = e0 - lj[0, j] * q
            e1 = e1 - lj[1, j] * q
        err[0] = e0
        err[1] = e1
        return e0, e1

    def cam_rows(i, k):
        return cj[i, 0:8, k, :]

    zero = jnp.zeros((1, 128), F32)
    e0, e1 = eliminate(rs[0], rs[1], 0)
    nat[0] = cj[0, 8] * e0 + cj[1, 8] * e1
    nat[1] = cj[0, 8] * cj[0, 8] + cj[1, 8] * cj[1, 8]
    for k in range(K):
        prepare(k, cam_rows(0, k) * err[0, k:k + 1, :] + cam_rows(1, k) * err[1, k:k + 1, :], nat[0, k:k + 1, :])
    scatter_half(0, 0, 1, zero)
    pl.semaphore_wait(barrier, len(others))
    start_core(0)
    scatter_half(0, 0, 0, zero)
    for k in range(K):
        c0, c1 = cam_rows(0, k), cam_rows(1, k)
        prepare(k, c0 * c0 + c1 * c1, nat[1, k:k + 1, :])
    scatter_half(1, 576, 1, zero)
    start_core(1)
    start_plane(0)
    scatter_half(1, 576, 0, zero)
    start_plane(1)

    for n in range(2):
        pair_buf[n, z % 2] = end_plane(n)
        push(pair_buf.at[n, z % 2], pair_buf.at[n, z % 2], s_zp.at[n], r_zp.at[n], at(x, c, y, pair))
        pending.append((pair_buf.at[n, 0], s_zp.at[n]))
    for n in range(2):
        landed(pair_buf.at[n, pair % 2], r_zp.at[n])
        even_buf[n, z // 2] = total(pair_buf.at[n], 2)
        for _, device in evens:
            push(even_buf.at[n, z // 2], even_buf.at[n, z // 2], s_ze.at[n], r_ze.at[n], device)
    drain()
    for n in range(2):
        landed(even_buf.at[n, pl.ds(0, 7)], r_ze.at[n])
        pending.append((even_buf.at[n, pl.ds(0, 7)], s_ze.at[n]))
    summed = [total(even_buf.at[n], 8) for n in range(2)]
    real = lax.broadcasted_iota(jnp.int32, (TILE, 128), 0) < 18
    scalar_row = lax.broadcasted_iota(jnp.int32, (TILE, 128), 0) == 18

    def inner(left, right):
        return jnp.sum(jnp.where(real, left * right, 0.0), keepdims=True)

    residual = jnp.where(real, summed[0], 0.0)
    diagonal = jnp.where(real, summed[1], 0.0) + DAMPING
    precond = residual / diagonal

    def rz_half(n, h):
        out = fields[n, h, 0, 18:19, :]
        for s in range(1, 16):
            out = out + fields[n, h, s, 18:19, :]
        return out

    def load_half(n, h):
        for s in range(16):
            part = fields[n, h, s]
            h0, l0 = split(part[0:8])
            h1, l1 = split(part[8:16])
            row = h * 288 + s * 16
            fld[row:row + 16, 0:128] = jnp.concatenate([h0, l0], axis=0).astype(BF16)
            fld[row:row + 16, 128:256] = jnp.concatenate([h1, l1], axis=0).astype(BF16)
        for b in range(2):
            high, low = split(fields[n, h, :, 16 + b, :])
            fld[h * 288 + 256:h * 288 + 272, b * 128:b * 128 + 128] = high.astype(BF16)
            fld[h * 288 + 272:h * 288 + 288, b * 128:b * 128 + 128] = low.astype(BF16)

    def pick_half(h, k):
        ks = pl.ds(k * LM, LM)
        out = jnp.dot(fld[h * 288:h * 288 + 288, :], onehot[:, ks], preferred_element_type=F32)
        tags = tag8[:, ks]
        if h:
            high, low = acc[0:8, ks], acc[8:16, ks]
        else:
            high, low = jnp.zeros((8, LM), F32), jnp.zeros((8, LM), F32)
        for s in range(16):
            hit = tags == h * 16 + s
            high = jnp.where(hit, out[s * 16:s * 16 + 8], high)
            low = jnp.where(hit, out[s * 16 + 8:s * 16 + 16], low)
        last = (out[256:272] + out[272:288]) * hot_q[h * 16:h * 16 + 16, ks].astype(F32)
        return high, low, last[0:8] + last[8:16]

    def apply(n, where, wait, flow):
        load_half(n, 0)
        for k in range(K):
            ks = pl.ds(k * LM, LM)
            high, low, last = pick_half(0, k)
            acc[0:8, ks] = high
            acc[8:16, ks] = low
            last_acc[:, ks] = last
        wait()
        load_half(n, 1)
        for k in range(K):
            high, low, last = pick_half(1, k)
            values = high + low
            for i in range(2):
                nat[i, k:k + 1, :] = rows_sum(cam_rows(i, k) * values)
            nat[2, k:k + 1, :] = rows_sum(last + last_acc[:, pl.ds(k * LM, LM)])
        a0 = nat[0] + cj[0, 8] * nat[2]
        a1 = nat[1] + cj[1, 8] * nat[2]
        if n:
            beta = jnp.concatenate([(rz_half(1, 0) + rz_half(1, 1)) / (rz_half(0, 0) + rz_half(0, 1))] * 4, axis=1)
            a0 = a0 + beta * first_a[0]
            a1 = a1 + beta * first_a[1]
        else:
            first_a[0] = a0
            first_a[1] = a1
        e0, e1 = eliminate(a0, a1, where)
        nat[0] = cj[0, 8] * e0 + cj[1, 8] * e1
        product = jnp.sum(a0 * e0 + a1 * e1, keepdims=True)
        for k in range(K):
            prepare(k, cam_rows(0, k) * err[0, k:k + 1, :] + cam_rows(1, k) * err[1, k:k + 1, :], nat[0, k:k + 1, :])
        product = jnp.broadcast_to(product, (1, 128))
        scatter_half(flow, 0, 1, product)
        start_core(flow)
        scatter_half(flow, 0, 0, product)
        start_plane(flow)

    start_gather(0, jnp.where(scalar_row, inner(residual, precond), precond))
    apply(0, 1, lambda: end_gather(0), 2)
    rz = rz_half(0, 0) + rz_half(0, 1)

    def square_half(h, scale):
        out = jnp.zeros((TILE, 128), F32)
        for s in range(16):
            part = fields[0, h, s] if scale is None else fields[1, h, s] + scale * fields[0, h, s]
            out = out + part * part
        return jnp.sum(jnp.where(real, out, 0.0), keepdims=True)

    square = square_half(0, None) + square_half(1, None)
    z_buf[z] = end_plane(2)
    for _, device in column:
        push(z_buf.at[z], z_buf.at[z], s_z.at[0], r_z.at[0], device)
    drain()
    direction = jnp.where(real, fields[0, 0, xy], 0.0)
    landed(z_buf.at[pl.ds(0, 15)], r_z.at[0])
    pending.append((z_buf.at[pl.ds(0, 15)], s_z.at[0]))
    image = total(z_buf, 16)
    alpha1 = rz / (image[18:19] + DAMPING * square)
    residual = residual - alpha1 * jnp.where(real, image + DAMPING * direction, 0.0)
    precond = residual / diagonal
    start_gather(1, jnp.where(scalar_row, inner(residual, precond), precond))

    apply(1, 2, lambda: end_gather(1), 3)
    rz_next = rz_half(1, 0) + rz_half(1, 1)
    beta = rz_next / rz

    square = square_half(0, beta) + square_half(1, beta)

    def swap(value):
        out = value
        for d in range(1, 8):
            moved = pltpu.roll(pltpu.roll(value, 16 * d, 1), 8 - d, 0)
            out = jnp.where((lane // 16 - iota_rows + 8) % 8 == d, moved, out)
        return out

    def pack(store, tile, scalar):
        for b in range(2):
            first = swap(tile[b * 8:b * 8 + 8])
            row = jnp.broadcast_to(tile[16 + b:17 + b], (8, 128))
            second = row
            for g in range(1, 8):
                second = jnp.where(iota_rows == g, pltpu.roll(row, 128 - 16 * g, 1), second)
            second = jnp.where(lane < 16, second, scalar)
            for g in range(8):
                store[b * 8 + g, 0:1, :] = first[g:g + 1]
                store[b * 8 + g, 1:2, :] = second[g:g + 1]

    direction2 = jnp.where(real, fields[1, 0, xy] + beta * direction, 0.0)
    for i, tile in enumerate((direction, direction2, residual)):
        pack(packed.at[i], tile, 0.0)

    own = end_plane(3)
    pack(slice_out, own, jnp.broadcast_to(own[18:19], (8, 128)))
    for slot, device in column:
        push(slice_out.at[slot], slice_in.at[z], s_z.at[1], r_z.at[1], device)
    slice_in[z] = slice_out[z]
    drain()
    landed(slice_in.at[pl.ds(0, 15)], r_z.at[1])
    image = total(slice_in, 16)
    pick = lax.broadcasted_iota(jnp.int32, (2, 128), 0) * 128 + lax.broadcasted_iota(jnp.int32, (2, 128), 1)
    product = jnp.sum(jnp.where(pick == 144, image, 0.0), keepdims=True)
    alpha2 = rz_next / (product + DAMPING * square)
    fin[group, 0:2, :] = alpha1 * packed[0, z] + alpha2 * packed[1, z]
    fin[group, 2:4, :] = packed[2, z] - alpha2 * (image + DAMPING * packed[1, z])

    for _, device in family:
        push(fin.at[group], fin.at[group], s_fin.at[0], r_fin.at[0], device)
    landed(slice_in.at[pl.ds(0, 15)], s_z.at[1])

    scale1 = jnp.concatenate([alpha1] * 4, axis=1)
    scale2 = jnp.concatenate([alpha2] * 4, axis=1)
    lm_o[...] = q_sc[0:3, :] - scale1 * q_sc[3:6, :] - scale2 * q_sc[6:9, :]
    landed(fin.at[pl.ds(0, 7)], r_fin.at[0])
    for i, out in enumerate((step_o, res_o)):
        out[0:8, :] = swap(fin[:, 2 * i, :])
        second = fin[:, 2 * i + 1, :]
        row = second[0:1]
        for g in range(1, 8):
            row = jnp.where(lane[0:1] // 16 == g, pltpu.roll(second, 16 * g, 1)[g:g + 1], row)
        out[8:9, :] = row
    landed(fin.at[pl.ds(0, 7)], s_fin.at[0])


def deliver(step, res, lm, step_o, res_o, lm_o):
    step_o[...] = step[...]
    res_o[...] = res[...]
    lm_o[...] = lm[...]


def body(cam_jac, lm_jac, resid, cam_index):
    vmem = pl.BlockSpec(memory_space=pltpu.VMEM)

    def tiles(*lead):
        return pltpu.VMEM(lead + (TILE, 128), F32)

    dma = pltpu.SemaphoreType.DMA
    scratch = [
        pltpu.VMEM((2, 9, K, LM), F32), pltpu.VMEM((2, 3, K, LM), F32), pltpu.VMEM((2, K, LM), F32), pltpu.VMEM((K, LM), jnp.int32),
        pltpu.VMEM((256, OBS), BF16), pltpu.VMEM((8, OBS), jnp.int32), pltpu.VMEM((16, OBS), BF16), pltpu.VMEM((32, OBS), BF16),
        pltpu.VMEM((16, OBS), BF16), pltpu.VMEM((2, OBS), F32), pltpu.VMEM((1152, OBS), BF16), pltpu.VMEM((576, 256), BF16),
        pltpu.VMEM((16, OBS), F32), pltpu.VMEM((8, OBS), F32),
        pltpu.VMEM((3, K, LM), F32), pltpu.VMEM((2, K, LM), F32), pltpu.VMEM((2, K, LM), F32), pltpu.VMEM((8, LM), F32), pltpu.VMEM((16, LM), F32),
        tiles(FLOWS, 2, 16), tiles(FLOWS, 16), tiles(FLOWS, 16), tiles(2, 2), tiles(2, 8), tiles(16),
        pltpu.VMEM((16, 2, 128), F32), pltpu.VMEM((16, 2, 128), F32), tiles(2, 2, 16), pltpu.VMEM((3, 16, 2, 128), F32),
        pltpu.VMEM((8, 4, 128), F32),
        dma((FLOWS,)), dma((FLOWS,)), dma((FLOWS,)), dma((FLOWS,)), dma((2,)), dma((2,)), dma((2,)), dma((2,)),
        dma((2,)), dma((2,)), dma((2,)), dma((2, 16)), dma((2,)), dma((2,)), dma((1,)), dma((1,)), dma((4,)),
    ]
    out_shape = (jax.ShapeDtypeStruct((9, 128), F32), jax.ShapeDtypeStruct((9, 128), F32), jax.ShapeDtypeStruct((3, LM), F32))
    results = pl.pallas_call(
        kernel,
        out_shape=(pltpu.VMEM((9, 128), F32), pltpu.VMEM((9, 128), F32), pltpu.VMEM((3, LM), F32)),
        in_specs=[pl.BlockSpec(memory_space=pl.ANY)] * 4,
        out_specs=(vmem, vmem, vmem),
        scratch_shapes=scratch,
        name="schur_cg",
        compiler_params=pltpu.CompilerParams(collective_id=0, has_side_effects=True, vmem_limit_bytes=60 << 20),
    )(cam_jac, lm_jac, resid, cam_index)
    return pl.pallas_call(
        deliver,
        out_shape=out_shape,
        in_specs=[vmem] * 3,
        out_specs=(vmem, vmem, vmem),
        name="deliver",
    )(*(pltpu.with_memory_space_constraint(r, pltpu.MemorySpace.VMEM) for r in results))


def solution(mesh):
    in_specs = (
        P(None, None, None, ("group", "dev")),
        P(None, None, None, ("group", "dev")),
        P(None, None, ("group", "dev")),
        P(None, ("group", "dev")),
    )
    out_specs = (P(None, "dev"), P(None, "dev"), P(None, ("group", "dev")))
    return jax.shard_map(body, mesh=mesh, in_specs=in_specs, out_specs=out_specs, check_vma=False)
```

```python
import functools

import jax
import jax.numpy as jnp
from jax import lax
from jax.experimental import pallas as pl
from jax.experimental.pallas import tpu as pltpu
from jax.sharding import PartitionSpec as P

DAMPING = 1.0
MESH = pl.DeviceIdType.MESH
F32 = jnp.float32
BF16 = jnp.bfloat16

TILE = 10
K = 8
LM = 512
OBS = K * LM
FLOWS = 3


def split(value):
    high = value.astype(BF16).astype(F32)
    return high, value - high


def rows_sum(value):
    return jnp.sum(value, axis=0, keepdims=True)


def total(buf, count):
    out = buf[0]
    for k in range(1, count):
        out = out + buf[k]
    return out


def kernel(cj_hbm, lj_hbm, rs_hbm, ci_hbm, step_o, res_o, lm_o,
           cj, lj, rs, ci, onehot, tag8, tag16, hot_q, both_sc, last_sc, lhs, fld, acc, last_acc, nat, first_a, err, inv, q_sc,
           terms, cores, plane_buf, terms1, cores1, plane1, even1, even2, slice_out, slice_in, fields, packed, fin,
           s_core, r_core, s_xy, r_xy, s_ze, r_ze, s_z, r_z, s_gx, r_gx, s_gc, r_gc, s_fin, r_fin, s_in):
    group = lax.axis_index("group")
    dev = lax.axis_index("dev")
    x, c = group // 2, group % 2
    z, y = dev // 4, dev % 4
    xy = x * 4 + y

    def at(xx, cc, yy, zz):
        return {"group": xx * 2 + cc, "dev": zz * 4 + yy}

    sibling = at(x, 1 - c, y, z)
    odd, level = z % 2, z // 2
    mine = odd * 16 + xy
    plane = []
    for k in (10, 6, 14, 9, 11, 2, 8, 5, 7, 13, 15, 1, 3, 4, 12, 0):
        xx, yy = (x + k // 4) % 4, (y + k % 4) % 4
        for o in (1, 0):
            if k or o:
                b = (odd + o) % 2
                plane.append((b * 16 + xx * 4 + yy, at(xx, c, yy, level * 2 + b)))
    evens = [((level + k) % 8, at(x, c, y, (z + 2 * k) % 16)) for k in (4, 3, 5, 2, 6, 1, 7)]
    family, cousins = [], []
    for k in (2, 1, 3, 0):
        for o in (1, 0):
            if k or o:
                xx, cc = (x + k) % 4, (c + o) % 2
                family.append((xx * 2 + cc, at(xx, cc, y, z)))
                if k and o:
                    cousins.append(at(xx, cc, y, z))

    loads = [pltpu.make_async_copy(a, b, s_in.at[i])
             for i, (a, b) in enumerate(((ci_hbm, ci), (lj_hbm, lj), (rs_hbm, rs), (cj_hbm, cj)))]
    for load in loads:
        load.start()

    barrier = pltpu.get_barrier_semaphore()
    others = [d for _, d in evens + plane] + cousins + [sibling]
    for d in others:
        pl.semaphore_signal(barrier, inc=1, device_id=d, device_id_type=MESH)

    loads[0].wait()

    iota256 = lax.broadcasted_iota(jnp.int32, (256, LM), 0)
    iota32 = lax.broadcasted_iota(jnp.int32, (32, LM), 0)
    for k in range(K):
        ks = pl.ds(k * LM, LM)
        cam = ci[k:k + 1, :]
        low = ((cam >> 9) & 1) * 128 + (cam >> 10) * 16 + (cam & 15)
        tag = (((cam >> 4) & 1) ^ c) * 16 + ((cam >> 5) & 3) * 4 + ((cam >> 7) & 3)
        onehot[:, ks] = jnp.where(iota256 == low, 1.0, 0.0).astype(BF16)
        hot_q[:, ks] = jnp.where(iota32 == tag, 1.0, 0.0).astype(BF16)
        tag8[:, ks] = jnp.broadcast_to(tag, (8, LM))
        tag16[:, ks] = jnp.broadcast_to(tag.astype(F32), (16, LM)).astype(BF16)

    def prepare(k, first8, last):
        ks = pl.ds(k * LM, LM)
        both_sc[:, ks] = jnp.concatenate(split(first8), axis=0).astype(BF16)
        high, low = split(last)
        last_sc[0:1, ks] = high
        last_sc[1:2, ks] = low

    def put_half(base, h):
        for k in range(K):
            ks = pl.ds(k * LM, LM)
            both = both_sc[:, ks]
            tags = tag16[:, ks]
            row = base + h * 288
            for q in range(16):
                lhs[row + q * 16:row + q * 16 + 16, ks] = jnp.where(tags == BF16(h * 16 + q), both, BF16(0))
            hot = hot_q[h * 16:h * 16 + 16, ks]
            lhs[row + 256:row + 272, ks] = hot * jnp.broadcast_to(last_sc[0:1, ks], (16, LM)).astype(BF16)
            lhs[row + 272:row + 288, ks] = hot * jnp.broadcast_to(last_sc[1:2, ks], (16, LM)).astype(BF16)

    def dot_t(left, right):
        return lax.dot_general(left, right, (((1,), (1,)), ((), ())), preferred_element_type=F32)

    iota_rows = lax.broadcasted_iota(jnp.int32, (8, 128), 0)
    lane = lax.broadcasted_iota(jnp.int32, (8, 128), 1)

    def scatter_half(out_terms, base, h, scalar):
        put_half(base, h)
        out = dot_t(lhs[base + h * 288:base + h * 288 + 288, :], onehot[...])
        last = out[256:272] + out[272:288]
        for q in range(16):
            both = out[q * 16:q * 16 + 8] + out[q * 16 + 8:q * 16 + 16]
            for b in range(2):
                out_terms(h, b * 16 + q)[0:8, :] = both[:, b * 128:b * 128 + 128]
                tail = jnp.where(iota_rows == 0, last[q:q + 1, b * 128:b * 128 + 128], scalar)
                out_terms(h, b * 16 + q)[8:10, :] = tail[0:2]

    pending = []

    def push(src, dst, send, recv, device):
        pltpu.make_async_remote_copy(
            src_ref=src, dst_ref=dst, send_sem=send, recv_sem=recv, device_id=device, device_id_type=MESH).start()

    def landed(dst, sem):
        pltpu.make_async_copy(dst, dst, sem).wait()

    def drain():
        while pending:
            landed(*pending.pop(0))

    flows = ((terms1, cores1, plane1), (terms.at[0], cores.at[0], plane_buf.at[0]), (terms.at[1], cores.at[1], plane_buf.at[1]))

    def start_core(n):
        source, store, _ = flows[n]
        push(source.at[1], store, s_core.at[n], r_core.at[n], sibling)
        pending.append((source.at[1], s_core.at[n]))

    def start_plane(n):
        source, store, spread = flows[n]
        landed(store, r_core.at[n])
        for slot in range(32):
            source[0, slot] = source[0, slot] + store[slot]
        for slot, device in plane:
            push(source.at[0, slot], spread.at[mine], s_xy.at[n], r_xy.at[n], device)
        pending.append((spread.at[pl.ds(0, 31)], s_xy.at[n]))
        spread[mine] = source[0, mine]

    def end_plane(n):
        spread = flows[n][2]
        landed(spread.at[pl.ds(0, 31)], r_xy.at[n])
        return total(spread, 32)

    def start_gather(n, tile):
        fields[n, 0, mine] = tile
        for slot, device in plane:
            push(fields.at[n, 0, mine], fields.at[n, 0, mine], s_gx.at[n], r_gx.at[n], device)
        pending.append((fields.at[n, 0, pl.ds(0, 31)], s_gx.at[n]))
        landed(fields.at[n, 0, pl.ds(0, 31)], r_gx.at[n])
        push(fields.at[n, 0], fields.at[n, 1], s_gc.at[n], r_gc.at[n], sibling)
        pending.append((fields.at[n, 0], s_gc.at[n]))

    def end_gather(n):
        landed(fields.at[n, 1], r_gc.at[n])

    def entry(first, second):
        return rows_sum(lj[0, first] * lj[0, second] + lj[1, first] * lj[1, second])

    loads[1].wait()
    loads[2].wait()
    loads[3].wait()
    w_00 = entry(0, 0) + DAMPING
    w_11 = entry(1, 1) + DAMPING
    w_22 = entry(2, 2) + DAMPING
    w_01 = entry(0, 1)
    w_02 = entry(0, 2)
    w_12 = entry(1, 2)
    cof_00 = w_11 * w_22 - w_12 * w_12
    cof_01 = w_02 * w_12 - w_01 * w_22
    cof_02 = w_01 * w_12 - w_02 * w_11
    cof_11 = w_00 * w_22 - w_02 * w_02
    cof_12 = w_01 * w_02 - w_00 * w_12
    cof_22 = w_00 * w_11 - w_01 * w_01
    determinant = w_00 * cof_00 + w_01 * cof_01 + w_02 * cof_02
    for i, cof in enumerate((cof_00, cof_01, cof_02, cof_11, cof_12, cof_22)):
        inv[i:i + 1, :] = cof / determinant

    def eliminate(a0, a1, where):
        side = [rows_sum(lj[0, j] * a0 + lj[1, j] * a1) for j in range(3)]
        picks = ((0, 1, 2), (1, 3, 4), (2, 4, 5))
        e0, e1 = a0, a1
        for j in range(3):
            q = sum(inv[p:p + 1, :] * side[m] for m, p in enumerate(picks[j]))
            q_sc[where * 3 + j:where * 3 + j + 1, :] = q
            e0 = e0 - lj[0, j] * q
            e1 = e1 - lj[1, j] * q
        err[0] = e0
        err[1] = e1
        return e0, e1

    def cam_rows(i, k):
        return cj[i, 0:8, k, :]

    zero = jnp.zeros((1, 128), F32)
    e0, e1 = eliminate(rs[0], rs[1], 0)
    nat[0] = cj[0, 8] * e0 + cj[1, 8] * e1
    nat[1] = cj[0, 8] * cj[0, 8] + cj[1, 8] * cj[1, 8]
    for k in range(K):
        prepare(k, cam_rows(0, k) * err[0, k:k + 1, :] + cam_rows(1, k) * err[1, k:k + 1, :], nat[0, k:k + 1, :])
    scatter_half(lambda h, q: terms1.at[h, q, 0], 0, 1, zero)
    scatter_half(lambda h, q: terms1.at[h, q, 0], 0, 0, zero)
    for k in range(K):
        c0, c1 = cam_rows(0, k), cam_rows(1, k)
        prepare(k, c0 * c0 + c1 * c1, nat[1, k:k + 1, :])
    scatter_half(lambda h, q: terms1.at[h, q, 1], 576, 1, zero)
    pl.semaphore_wait(barrier, len(others))
    start_core(0)
    scatter_half(lambda h, q: terms1.at[h, q, 1], 576, 0, zero)
    start_plane(0)

    even1[level] = end_plane(0)
    for _, device in evens:
        push(even1.at[level], even1.at[level], s_ze.at[0], r_ze.at[0], device)
    drain()
    landed(even1.at[pl.ds(0, 7)], r_ze.at[0])
    pending.append((even1.at[pl.ds(0, 7)], s_ze.at[0]))
    summed = total(even1, 8)
    real = lax.broadcasted_iota(jnp.int32, (TILE, 128), 0) < 9
    scalar_row = lax.broadcasted_iota(jnp.int32, (TILE, 128), 0) == 9

    def inner(left, right):
        return jnp.sum(jnp.where(real, left * right, 0.0), keepdims=True)

    residual = jnp.where(real, summed[0], 0.0)
    diagonal = jnp.where(real, summed[1], 0.0) + DAMPING
    precond = residual / diagonal

    def rz_half(n, h):
        out = fields[n, h, 0, 9:10, :]
        for s in range(1, 32):
            out = out + fields[n, h, s, 9:10, :]
        return out

    def load_half(n, h):
        for s in range(16):
            h0, l0 = split(fields[n, h, s, 0:8, :])
            h1, l1 = split(fields[n, h, 16 + s, 0:8, :])
            row = h * 288 + s * 16
            fld[row:row + 16, 0:128] = jnp.concatenate([h0, l0], axis=0).astype(BF16)
            fld[row:row + 16, 128:256] = jnp.concatenate([h1, l1], axis=0).astype(BF16)
        for b in range(2):
            high, low = split(fields[n, h, pl.ds(b * 16, 16), 8, :])
            fld[h * 288 + 256:h * 288 + 272, b * 128:b * 128 + 128] = high.astype(BF16)
            fld[h * 288 + 272:h * 288 + 288, b * 128:b * 128 + 128] = low.astype(BF16)

    def pick_half(h, k):
        ks = pl.ds(k * LM, LM)
        out = jnp.dot(fld[h * 288:h * 288 + 288, :], onehot[:, ks], preferred_element_type=F32)
        tags = tag8[:, ks]
        if h:
            high, low = acc[0:8, ks], acc[8:16, ks]
        else:
            high, low = jnp.zeros((8, LM), F32), jnp.zeros((8, LM), F32)
        for s in range(16):
            hit = tags == h * 16 + s
            high = jnp.where(hit, out[s * 16:s * 16 + 8], high)
            low = jnp.where(hit, out[s * 16 + 8:s * 16 + 16], low)
        last = (out[256:272] + out[272:288]) * hot_q[h * 16:h * 16 + 16, ks].astype(F32)
        return high, low, last[0:8] + last[8:16]

    def apply(n, where, wait, flow):
        load_half(n, 0)
        for k in range(K):
            ks = pl.ds(k * LM, LM)
            high, low, last = pick_half(0, k)
            acc[0:8, ks] = high
            acc[8:16, ks] = low
            last_acc[:, ks] = last
        wait()
        load_half(n, 1)
        for k in range(K):
            high, low, last = pick_half(1, k)
            values = high + low
            for i in range(2):
                nat[i, k:k + 1, :] = rows_sum(cam_rows(i, k) * values)
            nat[2, k:k + 1, :] = rows_sum(last + last_acc[:, pl.ds(k * LM, LM)])
        a0 = nat[0] + cj[0, 8] * nat[2]
        a1 = nat[1] + cj[1, 8] * nat[2]
        if n:
            beta = jnp.concatenate([(rz_half(1, 0) + rz_half(1, 1)) / (rz_half(0, 0) + rz_half(0, 1))] * 4, axis=1)
            a0 = a0 + beta * first_a[0]
            a1 = a1 + beta * first_a[1]
        else:
            first_a[0] = a0
            first_a[1] = a1
        e0, e1 = eliminate(a0, a1, where)
        nat[0] = cj[0, 8] * e0 + cj[1, 8] * e1
        product = jnp.sum(a0 * e0 + a1 * e1, keepdims=True)
        for k in range(K):
            prepare(k, cam_rows(0, k) * err[0, k:k + 1, :] + cam_rows(1, k) * err[1, k:k + 1, :], nat[0, k:k + 1, :])
        product = jnp.broadcast_to(product, (1, 128))
        scatter_half(lambda h, q: terms.at[flow - 1, h, q], 0, 1, product)
        start_core(flow)
        scatter_half(lambda h, q: terms.at[flow - 1, h, q], 0, 0, product)
        start_plane(flow)

    start_gather(0, jnp.where(scalar_row, inner(residual, precond), precond))
    apply(0, 1, lambda: end_gather(0), 1)
    rz = rz_half(0, 0) + rz_half(0, 1)

    def square_half(h, scale):
        out = jnp.zeros((TILE, 128), F32)
        for s in range(32):
            part = fields[0, h, s] if scale is None else fields[1, h, s] + scale * fields[0, h, s]
            out = out + part * part
        return jnp.sum(jnp.where(real, out, 0.0), keepdims=True)

    square = square_half(0, None) + square_half(1, None)
    even2[level] = end_plane(1)
    for _, device in evens:
        push(even2.at[level], even2.at[level], s_ze.at[1], r_ze.at[1], device)
    drain()
    direction = jnp.where(real, fields[0, 0, mine], 0.0)
    landed(even2.at[pl.ds(0, 7)], r_ze.at[1])
    pending.append((even2.at[pl.ds(0, 7)], s_ze.at[1]))
    image = total(even2, 8)
    alpha1 = rz / (image[9:10] + DAMPING * square)
    residual = residual - alpha1 * jnp.where(real, image + DAMPING * direction, 0.0)
    precond = residual / diagonal
    start_gather(1, jnp.where(scalar_row, inner(residual, precond), precond))

    apply(1, 2, lambda: end_gather(1), 2)
    rz_next = rz_half(1, 0) + rz_half(1, 1)
    beta = rz_next / rz

    square = square_half(0, beta) + square_half(1, beta)

    def swap(value):
        out = value
        for d in range(1, 8):
            moved = pltpu.roll(pltpu.roll(value, 16 * d, 1), 8 - d, 0)
            out = jnp.where((lane // 16 - iota_rows + 8) % 8 == d, moved, out)
        return out

    def pack(store, tile, scalar):
        first = swap(tile[0:8])
        row = jnp.broadcast_to(tile[8:9], (8, 128))
        second = row
        for g in range(1, 8):
            second = jnp.where(iota_rows == g, pltpu.roll(row, 128 - 16 * g, 1), second)
        second = jnp.where(lane < 16, second, scalar)
        for g in range(8):
            store[g, 0:1, :] = first[g:g + 1]
            store[g, 1:2, :] = second[g:g + 1]

    direction2 = jnp.where(real, fields[1, 0, mine] + beta * direction, 0.0)
    for i, tile in enumerate((direction, direction2, residual)):
        pack(packed.at[i], tile, 0.0)

    own = end_plane(2)
    pack(slice_out, own, jnp.broadcast_to(own[9:10], (8, 128)))
    for slot, device in evens:
        push(slice_out.at[slot], slice_in.at[level], s_z.at[0], r_z.at[0], device)
    slice_in[level] = slice_out[level]
    drain()
    landed(slice_in.at[pl.ds(0, 7)], r_z.at[0])
    image = total(slice_in, 8)
    pick = lax.broadcasted_iota(jnp.int32, (2, 128), 0) * 128 + lax.broadcasted_iota(jnp.int32, (2, 128), 1)
    product = jnp.sum(jnp.where(pick == 144, image, 0.0), keepdims=True)
    alpha2 = rz_next / (product + DAMPING * square)
    fin[group, 0:2, :] = alpha1 * packed[0, level] + alpha2 * packed[1, level]
    fin[group, 2:4, :] = packed[2, level] - alpha2 * (image + DAMPING * packed[1, level])

    for _, device in family:
        push(fin.at[group], fin.at[group], s_fin.at[0], r_fin.at[0], device)
    landed(slice_in.at[pl.ds(0, 7)], s_z.at[0])

    scale1 = jnp.concatenate([alpha1] * 4, axis=1)
    scale2 = jnp.concatenate([alpha2] * 4, axis=1)
    lm_o[...] = q_sc[0:3, :] - scale1 * q_sc[3:6, :] - scale2 * q_sc[6:9, :]
    landed(fin.at[pl.ds(0, 7)], r_fin.at[0])
    for i, out in enumerate((step_o, res_o)):
        out[0:8, :] = swap(fin[:, 2 * i, :])
        second = fin[:, 2 * i + 1, :]
        row = second[0:1]
        for g in range(1, 8):
            row = jnp.where(lane[0:1] // 16 == g, pltpu.roll(second, 16 * g, 1)[g:g + 1], row)
        out[8:9, :] = row
    landed(fin.at[pl.ds(0, 7)], s_fin.at[0])


def deliver(step, res, lm, step_o, res_o, lm_o):
    step_o[...] = step[...]
    res_o[...] = res[...]
    lm_o[...] = lm[...]


def body(cam_jac, lm_jac, resid, cam_index):
    vmem = pl.BlockSpec(memory_space=pltpu.VMEM)

    def tiles(*lead):
        return pltpu.VMEM(lead + (TILE, 128), F32)

    dma = pltpu.SemaphoreType.DMA
    scratch = [
        pltpu.VMEM((2, 9, K, LM), F32), pltpu.VMEM((2, 3, K, LM), F32), pltpu.VMEM((2, K, LM), F32), pltpu.VMEM((K, LM), jnp.int32),
        pltpu.VMEM((256, OBS), BF16), pltpu.VMEM((8, OBS), jnp.int32), pltpu.VMEM((16, OBS), BF16), pltpu.VMEM((32, OBS), BF16),
        pltpu.VMEM((16, OBS), BF16), pltpu.VMEM((2, OBS), F32), pltpu.VMEM((1152, OBS), BF16), pltpu.VMEM((576, 256), BF16),
        pltpu.VMEM((16, OBS), F32), pltpu.VMEM((8, OBS), F32),
        pltpu.VMEM((3, K, LM), F32), pltpu.VMEM((2, K, LM), F32), pltpu.VMEM((2, K, LM), F32), pltpu.VMEM((8, LM), F32), pltpu.VMEM((16, LM), F32),
        tiles(2, 2, 32), tiles(2, 32), tiles(2, 32), tiles(2, 32, 2), tiles(32, 2), tiles(32, 2), tiles(8, 2), tiles(8),
        pltpu.VMEM((8, 2, 128), F32), pltpu.VMEM((8, 2, 128), F32), tiles(2, 2, 32), pltpu.VMEM((3, 8, 2, 128), F32),
        pltpu.VMEM((8, 4, 128), F32),
        dma((FLOWS,)), dma((FLOWS,)), dma((FLOWS,)), dma((FLOWS,)), dma((2,)), dma((2,)), dma((1,)), dma((1,)),
        dma((2,)), dma((2,)), dma((2,)), dma((2,)), dma((1,)), dma((1,)), dma((4,)),
    ]
    out_shape = (jax.ShapeDtypeStruct((9, 128), F32), jax.ShapeDtypeStruct((9, 128), F32), jax.ShapeDtypeStruct((3, LM), F32))
    results = pl.pallas_call(
        kernel,
        out_shape=(pltpu.VMEM((9, 128), F32), pltpu.VMEM((9, 128), F32), pltpu.VMEM((3, LM), F32)),
        in_specs=[pl.BlockSpec(memory_space=pl.ANY)] * 4,
        out_specs=(vmem, vmem, vmem),
        scratch_shapes=scratch,
        name="schur_cg",
        compiler_params=pltpu.CompilerParams(collective_id=0, has_side_effects=True, vmem_limit_bytes=60 << 20),
    )(cam_jac, lm_jac, resid, cam_index)
    return pl.pallas_call(
        deliver,
        out_shape=out_shape,
        in_specs=[vmem] * 3,
        out_specs=(vmem, vmem, vmem),
        name="deliver",
    )(*(pltpu.with_memory_space_constraint(r, pltpu.MemorySpace.VMEM) for r in results))


def solution(mesh):
    in_specs = (
        P(None, None, None, ("group", "dev")),
        P(None, None, None, ("group", "dev")),
        P(None, None, ("group", "dev")),
        P(None, ("group", "dev")),
    )
    out_specs = (P(None, "dev"), P(None, "dev"), P(None, ("group", "dev")))
    return jax.shard_map(body, mesh=mesh, in_specs=in_specs, out_specs=out_specs, check_vma=False)
```

```python
import functools

import jax
import jax.numpy as jnp
from jax import lax
from jax.experimental import pallas as pl
from jax.experimental.pallas import tpu as pltpu
from jax.sharding import PartitionSpec as P

DAMPING = 1.0
MESH = pl.DeviceIdType.MESH
F32 = jnp.float32
BF16 = jnp.bfloat16

TILE = 10
K = 8
LM = 512
OBS = K * LM
FLOWS = 3


def split(value):
    high = value.astype(BF16).astype(F32)
    return high, value - high


def rows_sum(value):
    return jnp.sum(value, axis=0, keepdims=True)


def total(buf, count):
    out = buf[0]
    for k in range(1, count):
        out = out + buf[k]
    return out


def kernel(cj_hbm, lj_hbm, rs_hbm, ci_hbm, step_o, res_o, lm_o,
           cj, lj, rs, ci, onehot, tag8, tag16, hot_q, both_sc, last_sc, lhs, fld, acc, last_acc, nat, first_a, err, inv, q_sc,
           terms, cores, plane_buf, terms1, cores1, plane1, even1, even2, slice_out, slice_in, fields, packed, known, images, fin,
           s_core, r_core, s_xy, r_xy, s_ze, r_ze, s_z, r_z, s_gx, r_gx, s_gc, r_gc, s_fin, r_fin, s_img, r_img, s_in):
    group = lax.axis_index("group")
    dev = lax.axis_index("dev")
    x, c = group // 2, group % 2
    z, y = dev // 4, dev % 4
    xy = x * 4 + y

    def at(xx, cc, yy, zz):
        return {"group": xx * 2 + cc, "dev": zz * 4 + yy}

    sibling = at(x, 1 - c, y, z)
    odd, level = z % 2, z // 2
    mine = odd * 16 + xy
    plane = []
    for k in (10, 6, 14, 9, 11, 2, 8, 5, 7, 13, 15, 1, 3, 4, 12, 0):
        xx, yy = (x + k // 4) % 4, (y + k % 4) % 4
        for o in (1, 0):
            if k or o:
                b = (odd + o) % 2
                plane.append((b * 16 + xx * 4 + yy, at(xx, c, yy, level * 2 + b)))
    evens = [((level + k) % 8, at(x, c, y, (z + 2 * k) % 16)) for k in (4, 3, 5, 2, 6, 1, 7)]
    spots = []
    for k in (4, 3, 5, 2, 6, 1, 7, 0):
        for q in (2, 1, 3, 0):
            if k or q:
                spots.append(((level + k) % 8, at((x + q) % 4, c, y, (z + 2 * k) % 16), k and q))
    family, cousins = [], []
    for k in (2, 1, 3, 0):
        for o in (1, 0):
            if k or o:
                xx, cc = (x + k) % 4, (c + o) % 2
                family.append((xx * 2 + cc, at(xx, cc, y, z)))
                if k and o:
                    cousins.append(at(xx, cc, y, z))

    loads = [pltpu.make_async_copy(a, b, s_in.at[i])
             for i, (a, b) in enumerate(((ci_hbm, ci), (lj_hbm, lj), (rs_hbm, rs), (cj_hbm, cj)))]
    for load in loads:
        load.start()

    barrier = pltpu.get_barrier_semaphore()
    others = [d for _, d in evens + plane] + [d for _, d, far in spots if far] + cousins + [sibling]
    for d in others:
        pl.semaphore_signal(barrier, inc=1, device_id=d, device_id_type=MESH)

    loads[0].wait()

    iota256 = lax.broadcasted_iota(jnp.int32, (256, LM), 0)
    iota32 = lax.broadcasted_iota(jnp.int32, (32, LM), 0)
    for k in range(K):
        ks = pl.ds(k * LM, LM)
        cam = ci[k:k + 1, :]
        low = ((cam >> 9) & 1) * 128 + (cam >> 10) * 16 + (cam & 15)
        tag = (((cam >> 4) & 1) ^ c) * 16 + ((cam >> 5) & 3) * 4 + ((cam >> 7) & 3)
        onehot[:, ks] = jnp.where(iota256 == low, 1.0, 0.0).astype(BF16)
        hot_q[:, ks] = jnp.where(iota32 == tag, 1.0, 0.0).astype(BF16)
        tag8[:, ks] = jnp.broadcast_to(tag, (8, LM))
        tag16[:, ks] = jnp.broadcast_to(tag.astype(F32), (16, LM)).astype(BF16)

    def prepare(k, first8, last):
        ks = pl.ds(k * LM, LM)
        both_sc[:, ks] = jnp.concatenate(split(first8), axis=0).astype(BF16)
        high, low = split(last)
        last_sc[0:1, ks] = high
        last_sc[1:2, ks] = low

    def put_half(base, h):
        for k in range(K):
            ks = pl.ds(k * LM, LM)
            both = both_sc[:, ks]
            tags = tag16[:, ks]
            row = base + h * 288
            for q in range(16):
                lhs[row + q * 16:row + q * 16 + 16, ks] = jnp.where(tags == BF16(h * 16 + q), both, BF16(0))
            hot = hot_q[h * 16:h * 16 + 16, ks]
            lhs[row + 256:row + 272, ks] = hot * jnp.broadcast_to(last_sc[0:1, ks], (16, LM)).astype(BF16)
            lhs[row + 272:row + 288, ks] = hot * jnp.broadcast_to(last_sc[1:2, ks], (16, LM)).astype(BF16)

    def dot_t(left, right):
        return lax.dot_general(left, right, (((1,), (1,)), ((), ())), preferred_element_type=F32)

    iota_rows = lax.broadcasted_iota(jnp.int32, (8, 128), 0)
    lane = lax.broadcasted_iota(jnp.int32, (8, 128), 1)

    def scatter_half(out_terms, base, h, scalar):
        put_half(base, h)
        out = dot_t(lhs[base + h * 288:base + h * 288 + 288, :], onehot[...])
        last = out[256:272] + out[272:288]
        for q in range(16):
            both = out[q * 16:q * 16 + 8] + out[q * 16 + 8:q * 16 + 16]
            for b in range(2):
                out_terms(h, b * 16 + q)[0:8, :] = both[:, b * 128:b * 128 + 128]
                tail = jnp.where(iota_rows == 0, last[q:q + 1, b * 128:b * 128 + 128], scalar)
                out_terms(h, b * 16 + q)[8:10, :] = tail[0:2]

    pending = []

    def push(src, dst, send, recv, device):
        pltpu.make_async_remote_copy(
            src_ref=src, dst_ref=dst, send_sem=send, recv_sem=recv, device_id=device, device_id_type=MESH).start()

    def landed(dst, sem):
        pltpu.make_async_copy(dst, dst, sem).wait()

    def drain():
        while pending:
            landed(*pending.pop(0))

    flows = ((terms1, cores1, plane1), (terms.at[0], cores.at[0], plane_buf.at[0]), (terms.at[1], cores.at[1], plane_buf.at[1]))

    def start_core(n):
        source, store, _ = flows[n]
        push(source.at[1], store, s_core.at[n], r_core.at[n], sibling)
        pending.append((source.at[1], s_core.at[n]))

    def start_plane(n):
        source, store, spread = flows[n]
        landed(store, r_core.at[n])
        for slot in range(32):
            source[0, slot] = source[0, slot] + store[slot]
        for slot, device in plane:
            push(source.at[0, slot], spread.at[mine], s_xy.at[n], r_xy.at[n], device)
        pending.append((spread.at[pl.ds(0, 31)], s_xy.at[n]))
        spread[mine] = source[0, mine]

    def end_plane(n):
        spread = flows[n][2]
        landed(spread.at[pl.ds(0, 31)], r_xy.at[n])
        return total(spread, 32)

    def start_gather(n, tile):
        fields[n, 0, mine] = tile
        for slot, device in plane:
            push(fields.at[n, 0, mine], fields.at[n, 0, mine], s_gx.at[n], r_gx.at[n], device)
        pending.append((fields.at[n, 0, pl.ds(0, 31)], s_gx.at[n]))
        landed(fields.at[n, 0, pl.ds(0, 31)], r_gx.at[n])
        push(fields.at[n, 0], fields.at[n, 1], s_gc.at[n], r_gc.at[n], sibling)
        pending.append((fields.at[n, 0], s_gc.at[n]))

    def end_gather(n):
        landed(fields.at[n, 1], r_gc.at[n])

    def entry(first, second):
        return rows_sum(lj[0, first] * lj[0, second] + lj[1, first] * lj[1, second])

    loads[1].wait()
    loads[2].wait()
    loads[3].wait()
    w_00 = entry(0, 0) + DAMPING
    w_11 = entry(1, 1) + DAMPING
    w_22 = entry(2, 2) + DAMPING
    w_01 = entry(0, 1)
    w_02 = entry(0, 2)
    w_12 = entry(1, 2)
    cof_00 = w_11 * w_22 - w_12 * w_12
    cof_01 = w_02 * w_12 - w_01 * w_22
    cof_02 = w_01 * w_12 - w_02 * w_11
    cof_11 = w_00 * w_22 - w_02 * w_02
    cof_12 = w_01 * w_02 - w_00 * w_12
    cof_22 = w_00 * w_11 - w_01 * w_01
    determinant = w_00 * cof_00 + w_01 * cof_01 + w_02 * cof_02
    for i, cof in enumerate((cof_00, cof_01, cof_02, cof_11, cof_12, cof_22)):
        inv[i:i + 1, :] = cof / determinant

    def eliminate(a0, a1, where):
        side = [rows_sum(lj[0, j] * a0 + lj[1, j] * a1) for j in range(3)]
        picks = ((0, 1, 2), (1, 3, 4), (2, 4, 5))
        e0, e1 = a0, a1
        for j in range(3):
            q = sum(inv[p:p + 1, :] * side[m] for m, p in enumerate(picks[j]))
            q_sc[where * 3 + j:where * 3 + j + 1, :] = q
            e0 = e0 - lj[0, j] * q
            e1 = e1 - lj[1, j] * q
        err[0] = e0
        err[1] = e1
        return e0, e1

    def cam_rows(i, k):
        return cj[i, 0:8, k, :]

    zero = jnp.zeros((1, 128), F32)
    e0, e1 = eliminate(rs[0], rs[1], 0)
    nat[0] = cj[0, 8] * e0 + cj[1, 8] * e1
    nat[1] = cj[0, 8] * cj[0, 8] + cj[1, 8] * cj[1, 8]
    for k in range(K):
        prepare(k, cam_rows(0, k) * err[0, k:k + 1, :] + cam_rows(1, k) * err[1, k:k + 1, :], nat[0, k:k + 1, :])
    scatter_half(lambda h, q: terms1.at[h, q, 0], 0, 1, zero)
    scatter_half(lambda h, q: terms1.at[h, q, 0], 0, 0, zero)
    for k in range(K):
        c0, c1 = cam_rows(0, k), cam_rows(1, k)
        prepare(k, c0 * c0 + c1 * c1, nat[1, k:k + 1, :])
    scatter_half(lambda h, q: terms1.at[h, q, 1], 576, 1, zero)
    pl.semaphore_wait(barrier, len(others))
    start_core(0)
    scatter_half(lambda h, q: terms1.at[h, q, 1], 576, 0, zero)
    start_plane(0)

    even1[level] = end_plane(0)
    for _, device in evens:
        push(even1.at[level], even1.at[level], s_ze.at[0], r_ze.at[0], device)
    drain()
    landed(even1.at[pl.ds(0, 7)], r_ze.at[0])
    pending.append((even1.at[pl.ds(0, 7)], s_ze.at[0]))
    summed = total(even1, 8)
    real = lax.broadcasted_iota(jnp.int32, (TILE, 128), 0) < 9
    scalar_row = lax.broadcasted_iota(jnp.int32, (TILE, 128), 0) == 9

    def inner(left, right):
        return jnp.sum(jnp.where(real, left * right, 0.0), keepdims=True)

    residual = jnp.where(real, summed[0], 0.0)
    diagonal = jnp.where(real, summed[1], 0.0) + DAMPING
    precond = residual / diagonal

    def rz_half(n, h):
        out = fields[n, h, 0, 9:10, :]
        for s in range(1, 32):
            out = out + fields[n, h, s, 9:10, :]
        return out

    def load_half(n, h):
        for s in range(16):
            h0, l0 = split(fields[n, h, s, 0:8, :])
            h1, l1 = split(fields[n, h, 16 + s, 0:8, :])
            row = h * 288 + s * 16
            fld[row:row + 16, 0:128] = jnp.concatenate([h0, l0], axis=0).astype(BF16)
            fld[row:row + 16, 128:256] = jnp.concatenate([h1, l1], axis=0).astype(BF16)
        for b in range(2):
            high, low = split(fields[n, h, pl.ds(b * 16, 16), 8, :])
            fld[h * 288 + 256:h * 288 + 272, b * 128:b * 128 + 128] = high.astype(BF16)
            fld[h * 288 + 272:h * 288 + 288, b * 128:b * 128 + 128] = low.astype(BF16)

    def pick_half(h, k):
        ks = pl.ds(k * LM, LM)
        out = jnp.dot(fld[h * 288:h * 288 + 288, :], onehot[:, ks], preferred_element_type=F32)
        tags = tag8[:, ks]
        if h:
            high, low = acc[0:8, ks], acc[8:16, ks]
        else:
            high, low = jnp.zeros((8, LM), F32), jnp.zeros((8, LM), F32)
        for s in range(16):
            hit = tags == h * 16 + s
            high = jnp.where(hit, out[s * 16:s * 16 + 8], high)
            low = jnp.where(hit, out[s * 16 + 8:s * 16 + 16], low)
        last = (out[256:272] + out[272:288]) * hot_q[h * 16:h * 16 + 16, ks].astype(F32)
        return high, low, last[0:8] + last[8:16]

    def apply(n, where, wait, flow):
        load_half(n, 0)
        for k in range(K):
            ks = pl.ds(k * LM, LM)
            high, low, last = pick_half(0, k)
            acc[0:8, ks] = high
            acc[8:16, ks] = low
            last_acc[:, ks] = last
        wait()
        load_half(n, 1)
        for k in range(K):
            high, low, last = pick_half(1, k)
            values = high + low
            for i in range(2):
                nat[i, k:k + 1, :] = rows_sum(cam_rows(i, k) * values)
            nat[2, k:k + 1, :] = rows_sum(last + last_acc[:, pl.ds(k * LM, LM)])
        a0 = nat[0] + cj[0, 8] * nat[2]
        a1 = nat[1] + cj[1, 8] * nat[2]
        if n:
            beta = jnp.concatenate([(rz_half(1, 0) + rz_half(1, 1)) / (rz_half(0, 0) + rz_half(0, 1))] * 4, axis=1)
            a0 = a0 + beta * first_a[0]
            a1 = a1 + beta * first_a[1]
        else:
            first_a[0] = a0
            first_a[1] = a1
        e0, e1 = eliminate(a0, a1, where)
        nat[0] = cj[0, 8] * e0 + cj[1, 8] * e1
        product = jnp.sum(a0 * e0 + a1 * e1, keepdims=True)
        for k in range(K):
            prepare(k, cam_rows(0, k) * err[0, k:k + 1, :] + cam_rows(1, k) * err[1, k:k + 1, :], nat[0, k:k + 1, :])
        product = jnp.broadcast_to(product, (1, 128))
        scatter_half(lambda h, q: terms.at[flow - 1, h, q], 0, 1, product)
        start_core(flow)
        scatter_half(lambda h, q: terms.at[flow - 1, h, q], 0, 0, product)
        start_plane(flow)

    start_gather(0, jnp.where(scalar_row, inner(residual, precond), precond))
    apply(0, 1, lambda: end_gather(0), 1)
    rz = rz_half(0, 0) + rz_half(0, 1)

    def square_half(h, scale):
        out = jnp.zeros((TILE, 128), F32)
        for s in range(32):
            part = fields[0, h, s] if scale is None else fields[1, h, s] + scale * fields[0, h, s]
            out = out + part * part
        return jnp.sum(jnp.where(real, out, 0.0), keepdims=True)

    square = square_half(0, None) + square_half(1, None)
    even2[level] = end_plane(1)
    for _, device in evens:
        push(even2.at[level], even2.at[level], s_ze.at[1], r_ze.at[1], device)
    drain()
    direction = jnp.where(real, fields[0, 0, mine], 0.0)
    landed(even2.at[pl.ds(0, 7)], r_ze.at[1])
    pending.append((even2.at[pl.ds(0, 7)], s_ze.at[1]))
    image = total(even2, 8)
    alpha1 = rz / (image[9:10] + DAMPING * square)
    residual = residual - alpha1 * jnp.where(real, image + DAMPING * direction, 0.0)
    precond = residual / diagonal
    start_gather(1, jnp.where(scalar_row, inner(residual, precond), precond))

    apply(1, 2, lambda: end_gather(1), 2)
    rz_next = rz_half(1, 0) + rz_half(1, 1)
    beta = rz_next / rz

    square = square_half(0, beta) + square_half(1, beta)

    def swap(value):
        out = value
        for d in range(1, 8):
            moved = pltpu.roll(pltpu.roll(value, 16 * d, 1), 8 - d, 0)
            out = jnp.where((lane // 16 - iota_rows + 8) % 8 == d, moved, out)
        return out

    def pack(store, tile, scalar):
        first = swap(tile[0:8])
        row = jnp.broadcast_to(tile[8:9], (8, 128))
        second = row
        for g in range(1, 8):
            second = jnp.where(iota_rows == g, pltpu.roll(row, 128 - 16 * g, 1), second)
        second = jnp.where(lane < 16, second, scalar)
        for g in range(8):
            store[g, 0:1, :] = first[g:g + 1]
            store[g, 1:2, :] = second[g:g + 1]

    direction2 = jnp.where(real, fields[1, 0, mine] + beta * direction, 0.0)
    for i, tile in enumerate((direction, direction2, residual)):
        pack(packed.at[i], tile, 0.0)

    for i in range(3):
        known[group, 2 * i:2 * i + 2, :] = packed[i, level]
    for _, device in family:
        push(known.at[group], known.at[group], s_fin.at[0], r_fin.at[0], device)

    own = end_plane(2)
    pack(slice_out, own, jnp.broadcast_to(own[9:10], (8, 128)))
    for slot, device, _ in spots:
        push(slice_out.at[slot], slice_in.at[x * 8 + level], s_z.at[0], r_z.at[0], device)
    slice_in[x * 8 + level] = slice_out[level]
    drain()
    landed(known.at[pl.ds(0, 7)], s_fin.at[0])
    landed(known.at[pl.ds(0, 7)], r_fin.at[0])
    landed(slice_in.at[pl.ds(0, 31)], r_z.at[0])
    for k in range(4):
        image = slice_in[k * 8]
        for g in range(1, 8):
            image = image + slice_in[k * 8 + g]
        images[c, k] = image

    push(images.at[c], images.at[c], s_img.at[0], r_img.at[0], sibling)
    pick = lax.broadcasted_iota(jnp.int32, (2, 128), 0) * 128 + lax.broadcasted_iota(jnp.int32, (2, 128), 1)
    product = jnp.sum(jnp.where(pick == 144, images[c, 0], 0.0), keepdims=True)
    alpha2 = rz_next / (product + DAMPING * square)
    scale1 = jnp.concatenate([alpha1] * 4, axis=1)
    scale2 = jnp.concatenate([alpha2] * 4, axis=1)
    lm_o[...] = q_sc[0:3, :] - scale1 * q_sc[3:6, :] - scale2 * q_sc[6:9, :]
    for g in range(8):
        fin[g, 0:2, :] = alpha1 * known[g, 0:2, :] + alpha2 * known[g, 2:4, :]
    landed(slice_in.at[pl.ds(0, 31)], s_z.at[0])
    landed(images.at[0], r_img.at[0])
    for g in range(8):
        fin[g, 2:4, :] = known[g, 4:6, :] - alpha2 * (images[g % 2, g // 2] + DAMPING * known[g, 2:4, :])

    for i, out in enumerate((step_o, res_o)):
        out[0:8, :] = swap(fin[:, 2 * i, :])
        second = fin[:, 2 * i + 1, :]
        row = second[0:1]
        for g in range(1, 8):
            row = jnp.where(lane[0:1] // 16 == g, pltpu.roll(second, 16 * g, 1)[g:g + 1], row)
        out[8:9, :] = row
    landed(images.at[0], s_img.at[0])


def deliver(step, res, lm, step_o, res_o, lm_o):
    step_o[...] = step[...]
    res_o[...] = res[...]
    lm_o[...] = lm[...]


def body(cam_jac, lm_jac, resid, cam_index):
    vmem = pl.BlockSpec(memory_space=pltpu.VMEM)

    def tiles(*lead):
        return pltpu.VMEM(lead + (TILE, 128), F32)

    dma = pltpu.SemaphoreType.DMA
    scratch = [
        pltpu.VMEM((2, 9, K, LM), F32), pltpu.VMEM((2, 3, K, LM), F32), pltpu.VMEM((2, K, LM), F32), pltpu.VMEM((K, LM), jnp.int32),
        pltpu.VMEM((256, OBS), BF16), pltpu.VMEM((8, OBS), jnp.int32), pltpu.VMEM((16, OBS), BF16), pltpu.VMEM((32, OBS), BF16),
        pltpu.VMEM((16, OBS), BF16), pltpu.VMEM((2, OBS), F32), pltpu.VMEM((1152, OBS), BF16), pltpu.VMEM((576, 256), BF16),
        pltpu.VMEM((16, OBS), F32), pltpu.VMEM((8, OBS), F32),
        pltpu.VMEM((3, K, LM), F32), pltpu.VMEM((2, K, LM), F32), pltpu.VMEM((2, K, LM), F32), pltpu.VMEM((8, LM), F32), pltpu.VMEM((16, LM), F32),
        tiles(2, 2, 32), tiles(2, 32), tiles(2, 32), tiles(2, 32, 2), tiles(32, 2), tiles(32, 2), tiles(8, 2), tiles(8),
        pltpu.VMEM((8, 2, 128), F32), pltpu.VMEM((32, 2, 128), F32), tiles(2, 2, 32), pltpu.VMEM((3, 8, 2, 128), F32),
        pltpu.VMEM((8, 6, 128), F32), pltpu.VMEM((2, 4, 2, 128), F32),
        pltpu.VMEM((8, 4, 128), F32),
        dma((FLOWS,)), dma((FLOWS,)), dma((FLOWS,)), dma((FLOWS,)), dma((2,)), dma((2,)), dma((1,)), dma((1,)),
        dma((2,)), dma((2,)), dma((2,)), dma((2,)), dma((1,)), dma((1,)), dma((1,)), dma((1,)), dma((4,)),
    ]
    out_shape = (jax.ShapeDtypeStruct((9, 128), F32), jax.ShapeDtypeStruct((9, 128), F32), jax.ShapeDtypeStruct((3, LM), F32))
    results = pl.pallas_call(
        kernel,
        out_shape=(pltpu.VMEM((9, 128), F32), pltpu.VMEM((9, 128), F32), pltpu.VMEM((3, LM), F32)),
        in_specs=[pl.BlockSpec(memory_space=pl.ANY)] * 4,
        out_specs=(vmem, vmem, vmem),
        scratch_shapes=scratch,
        name="schur_cg",
        compiler_params=pltpu.CompilerParams(collective_id=0, has_side_effects=True, vmem_limit_bytes=60 << 20),
    )(cam_jac, lm_jac, resid, cam_index)
    return pl.pallas_call(
        deliver,
        out_shape=out_shape,
        in_specs=[vmem] * 3,
        out_specs=(vmem, vmem, vmem),
        name="deliver",
    )(*(pltpu.with_memory_space_constraint(r, pltpu.MemorySpace.VMEM) for r in results))


def solution(mesh):
    in_specs = (
        P(None, None, None, ("group", "dev")),
        P(None, None, None, ("group", "dev")),
        P(None, None, ("group", "dev")),
        P(None, ("group", "dev")),
    )
    out_specs = (P(None, "dev"), P(None, "dev"), P(None, ("group", "dev")))
    return jax.shard_map(body, mesh=mesh, in_specs=in_specs, out_specs=out_specs, check_vma=False)
```
